32 devices in a mesh: groups: 2 (over x), along: 8 (over z, y), across: 2 (over core).
Axes of the slice: x: 2, y: 2, z: 4, core: 2. Of those that a mesh axis runs over, the one named last changes fastest.
Arguments:
- toa_bands: bfloat16 [1024, 4, 2048], P(('groups', 'along'), None, 'across'), parts along dimension 0, may hold values from 0.019897461 to 0.59765625
- dark_mask: int32 [1024, 2048], P(('groups', 'along'), 'across'), parts along dimension 0, may hold values 0 or 1
- vapour: float32 [1024, 2048], P(('groups', 'along'), 'across'), parts along dimension 0, may hold values from 0 to 7
- elev_class: int32 [1024, 2048], P(('groups', 'along'), 'across'), parts along dimension 0, may hold values from 0 to 6
- elev_frac: float32 [1024, 2048], P(('groups', 'along'), 'across'), parts along dimension 0, may hold values from 0 to 1
- kernel: float32 [61], replicated, may hold values from 0.1 to 1
- lut_gain: bfloat16 [4, 8, 16, 8], replicated, may hold values from 1 to 2
- lut_path: bfloat16 [4, 8, 16, 8], replicated, may hold values from 0 to 0.29882812
- lut_albedo: bfloat16 [4, 8, 16, 8], replicated, may hold values from 0.049804688 to 0.25
- routes: int32 [64, 2], P(('groups', 'along')), parts along dimension 0, may hold values from 0 to 7, as said below
- starts: int32 [64, 2], P(('groups', 'along')), parts along dimension 0, may hold values from 0 to 48
Outputs:
- tile_out: bfloat16 [16, 64, 4, 2048], P(('groups', 'along'), None, None, 'across'), parts along dimension 0
The draws below stay inside these ranges and needn't reach their ends.
There are 2 independent parts, one for each index of `groups`. The reference program is written for one: setup_inputs(seed, part) draws one part's arguments, and reference() takes and returns one part's arrays. A program takes and returns all parts, laid end to end along the dimension named above; an argument that names none is the same for every part. Nothing has to cross between parts.
Inputs may be any that keep to these rules, and one draw needn't show every extreme that they name: `dark_mask`: 1 marks a dark pixel. `elev_class`: the class and the next one are both classes of the table. `routes`: the first block of segment s is s // 4, the block of the segment's own rows; the second lies 1 to 2 blocks before or after it; among the 4 segments of one device at most 2 have their second block at any one signed distance, and in every draw some device has exactly 2 at some distance.
All inputs are finite; a program needn't handle non-finite values. No bound on the sum of `dark_mask` on one device may be relied on, other than what follows from the above.
Results may differ from the reference program's by a relative error of at most 0.0043.
Values may be sent and summed in bfloat16 or wider, within the bound.
No kernel may reach another device: no remote copies, remote signals or barrier semaphores. Data moves between devices by JAX's collectives and lax.ppermute only.
A program may use at most 64 MiB of HBM per device.

```python
import math
import jax
import jax.numpy as jnp
from jax import lax

BANDS = 4
NA = 16
NW = 8
NE = 8
HALO = 30
SEG = 16
REACH = 2
ROW_DEV = 64
NR = 512
NC = 2048
SEG_DEV = 4
CAP = 2
NSEGS = 32
TILES = 8
TILE_ROWS = 64


def draw_routes(key, part):
    key_full = jax.random.fold_in(key, 101)
    key_slots = jax.random.fold_in(key, 202)
    key_order = jax.random.fold_in(key, 303)
    side_count = 2 * REACH
    side_ids = jnp.arange(side_count, dtype=jnp.int32)
    side_value = jnp.where(side_ids < REACH, side_ids - REACH, side_ids - REACH + 1)
    devices = jnp.arange(TILES, dtype=jnp.int32)
    dest = devices[:, None] + side_value[None, :]
    valid = (dest >= 0) & (dest < TILES)
    full_score = jax.random.randint(key_full, (TILES, side_count), 0, 1 << 16) * side_count + side_ids[None, :]
    full_side = jnp.argmax(jnp.where(valid, full_score, -1), axis=1).astype(jnp.int32)
    slot_ids = jnp.arange(side_count * CAP, dtype=jnp.int32)
    slot_side = slot_ids // CAP
    slot_score = jax.random.randint(key_slots, (TILES, side_count * CAP), 0, 1 << 16) * (side_count * CAP) + slot_ids[None, :]
    slot_valid = valid[:, slot_side]
    order_key = slot_score + (1 << 23) * (slot_side[None, :] != full_side[:, None]).astype(jnp.int32) + (1 << 25) * (1 - slot_valid.astype(jnp.int32))
    order = jnp.argsort(order_key, axis=1)[:, :SEG_DEV]
    chosen_side = slot_side[order]
    mix_score = jax.random.randint(key_order, (TILES, SEG_DEV), 0, 1 << 16) * SEG_DEV + jnp.arange(SEG_DEV, dtype=jnp.int32)[None, :]
    mix = jnp.argsort(mix_score, axis=1)
    chosen_side = jnp.take_along_axis(chosen_side, mix, axis=1)
    second = devices[:, None] + side_value[chosen_side]
    first = jnp.broadcast_to(devices[:, None], (TILES, SEG_DEV))
    return jnp.stack([first, second], axis=-1).reshape(NSEGS, 2).astype(jnp.int32)


def set_ends(entries, own_key, smallest, largest):
    shape = entries.shape
    index_at = [jax.random.randint(jax.random.fold_in(own_key, axis), (), 0, shape[axis]) for axis in range(len(shape))]
    entries = entries.at[tuple(index_at)].set(smallest)
    longest = shape.index(max(shape))
    index_at[longest] = (index_at[longest] + 1) % shape[longest]
    return entries.at[tuple(index_at)].set(largest)


def block_scale(rng, extent, split, least, top_value):
    gain = 1.0
    for position, parts in split:
        draws = jax.random.uniform(jax.random.fold_in(jax.random.fold_in(rng, 6), position), (parts,), jnp.float32, least / len(split), top_value / len(split))
        gain = gain * jnp.repeat(jnp.exp(draws), extent[position] // parts).reshape((-1,) + (1,) * (len(extent) - 1 - position))
    return gain


def setup_inputs(seed: int = 0, part: int = 0) -> dict:
    keys = jax.random.split(jax.random.key(seed), 12)
    part_splits = jax.random.split(jax.random.fold_in(keys[11], part), 12)
    return {
        "toa_bands": jnp.clip(0.019897461 + 0.5777588 * jax.random.uniform(part_splits[0], (NR, BANDS, NC), jnp.float32) ** block_scale(part_splits[0], (NR, BANDS, NC), ((0, 8), (2, 2)), -0.2, 0.2), 0.019897461, 0.59765625).astype(jnp.bfloat16),
        "dark_mask": set_ends((jax.random.randint(part_splits[1], (NR, NC), 0, 1024) < 1).astype(jnp.int32), jax.random.fold_in(part_splits[1], 1), 0, 1),
        "vapour": jnp.clip(7.0 * jax.random.uniform(part_splits[2], (NR, NC), jnp.float32) ** block_scale(part_splits[2], (NR, NC), ((0, 8), (1, 2)), -0.2, 0.2), 0.0, 7.0),
        "elev_class": set_ends(jax.random.randint(part_splits[3], (NR, NC), 0, NE - 1), jax.random.fold_in(part_splits[3], 1), 0, (NE - 1) - 1).astype(jnp.int32),
        "elev_frac": jnp.clip(1.0 * jax.random.uniform(part_splits[4], (NR, NC), jnp.float32) ** block_scale(part_splits[4], (NR, NC), ((0, 8), (1, 2)), -0.2, 0.2), 0.0, 1.0),
        "kernel": jnp.clip(jnp.exp(jax.random.uniform(keys[5], (2 * HALO + 1,), jnp.float32, math.log(0.1), math.log(1.0))), 0.1, 1.0),
        "lut_gain": jnp.clip(jax.random.uniform(keys[6], (BANDS, NE, NA, NW), jnp.float32, 1.0, 2.0), 1.0, 2.0).astype(jnp.bfloat16),
        "lut_path": jnp.clip(jax.random.uniform(keys[7], (BANDS, NE, NA, NW), jnp.float32, 0.0, 0.29882812), 0.0, 0.29882812).astype(jnp.bfloat16),
        "lut_albedo": jnp.clip(jax.random.uniform(keys[8], (BANDS, NE, NA, NW), jnp.float32, 0.049804688, 0.25), 0.049804688, 0.25).astype(jnp.bfloat16),
        "routes": draw_routes(jax.random.fold_in(jax.random.fold_in(keys[11], part), 71), part),
        "starts": set_ends(jax.random.randint(part_splits[10], (NSEGS, 2), 0, TILE_ROWS - SEG + 1), jax.random.fold_in(part_splits[10], 1), 0, TILE_ROWS - SEG).astype(jnp.int32),
    }


def smooth_axis(fields, kernel, axis):
    size = fields.shape[axis]
    tap_count = kernel.shape[0]
    half_width = tap_count // 2
    padding = [(0, 0), (0, 0), (0, 0)]
    padding[axis] = (half_width, half_width)
    padded = jnp.pad(fields, padding)
    total = jnp.zeros_like(fields)
    for tap in range(tap_count):
        total = total + kernel[tap] * lax.slice_in_dim(padded, tap, tap + size, axis=axis)
    return total


def correct_block(inputs, lut_table):
    toa_block, aero_pos, vapour_block, class_block, frac_block = inputs
    a_low = jnp.clip(jnp.floor(aero_pos).astype(jnp.int32), 0, NA - 2)
    a_frac = aero_pos - a_low.astype(aero_pos.dtype)
    w_low = jnp.clip(jnp.floor(vapour_block).astype(jnp.int32), 0, NW - 2)
    w_frac = vapour_block - w_low.astype(vapour_block.dtype)
    coefficient = jnp.zeros((lut_table.shape[0],) + aero_pos.shape, dtype=jnp.float32)
    for e_step in range(2):
        elev_weight = frac_block if e_step == 1 else 1.0 - frac_block
        for a_step in range(2):
            a_weight = a_frac if a_step == 1 else 1.0 - a_frac
            for w_step in range(2):
                w_weight = w_frac if w_step == 1 else 1.0 - w_frac
                joint_weight = (a_weight * w_weight).astype(jnp.bfloat16)
                joint_weight = lax.optimization_barrier(joint_weight).astype(jnp.float32)
                flat_index = ((class_block + e_step) * NA + a_low + a_step) * NW + w_low + w_step
                values = jnp.take(lut_table, flat_index.reshape(-1).astype(jnp.int32), axis=1)
                values = values.reshape((lut_table.shape[0],) + aero_pos.shape)
                coefficient = coefficient + (elev_weight * joint_weight)[None] * values
    coefficient = coefficient.reshape((BANDS, 3) + aero_pos.shape)
    radiance = jnp.transpose(toa_block.astype(jnp.float32), (1, 0, 2))
    scaled = coefficient[:, 0] * radiance - coefficient[:, 1]
    surface = scaled / (1.0 + coefficient[:, 2] * scaled)
    return jnp.transpose(surface, (1, 0, 2)).astype(jnp.bfloat16)


def reference(toa_bands, dark_mask, vapour, elev_class, elev_frac, kernel, lut_gain, lut_path, lut_albedo, routes, starts):
    darkness = dark_mask.astype(jnp.float32)
    blue_band = toa_bands[:, 0, :].astype(jnp.float32)
    red_band = toa_bands[:, 2, :].astype(jnp.float32)
    fields = jnp.stack([darkness * 8.0 * (blue_band - 0.5 * red_band), darkness])
    smoothed = smooth_axis(smooth_axis(fields, kernel, 1), kernel, 2)
    aerosol = smoothed[0] / jnp.maximum(smoothed[1], 1.0)
    aero_pos = (NA - 1) * jax.nn.sigmoid(aerosol)
    lut_table = jnp.stack([lut_gain, lut_path, lut_albedo], axis=1).astype(jnp.float32).reshape(BANDS * 3, NE * NA * NW)
    block_count = NR // ROW_DEV
    inputs = (toa_bands.reshape(block_count, ROW_DEV, BANDS, NC),
              aero_pos.reshape(block_count, ROW_DEV, NC),
              vapour.reshape(block_count, ROW_DEV, NC),
              elev_class.reshape(block_count, ROW_DEV, NC),
              elev_frac.reshape(block_count, ROW_DEV, NC))
    corrected = lax.map(lambda item: correct_block(item, lut_table), inputs).reshape(NR, BANDS, NC)
    segment_rows = corrected.reshape(NSEGS * SEG, BANDS * NC).astype(jnp.float32)
    summed = jnp.zeros((TILES * TILE_ROWS, BANDS * NC), dtype=jnp.float32)
    counts = jnp.zeros((TILES * TILE_ROWS,), dtype=jnp.float32)
    for route_slot in range(2):
        target = routes[:, route_slot][:, None] * TILE_ROWS + starts[:, route_slot][:, None] + jnp.arange(SEG, dtype=jnp.int32)[None, :]
        target = target.reshape(-1).astype(jnp.int32)
        summed = summed.at[target].add(segment_rows)
        counts = counts.at[target].add(jnp.ones((NSEGS * SEG,), dtype=jnp.float32))
    tile_out = (summed / jnp.maximum(counts, 1.0)[:, None]).astype(jnp.bfloat16)
    return tile_out.reshape(TILES, TILE_ROWS, BANDS, NC)
```

```python
import functools

import jax
import jax.numpy as jnp
from jax import lax
from jax.experimental import pallas as pl
from jax.experimental.pallas import tpu as pltpu
from jax.sharding import PartitionSpec as P

SEG = 16
CAP = 2
LANES = 128

F32 = jnp.float32
BF16 = jnp.bfloat16
VMEM = pl.BlockSpec(memory_space=pltpu.VMEM)
SMEM = pl.BlockSpec(memory_space=pltpu.SMEM)


def params(mib=32):
    return pltpu.CompilerParams(vmem_limit_bytes=mib * 1024 * 1024)


def swap_pairs(count, step, offset):
    pairs = []
    for i in range(count - step):
        if (i // step) % 2 == offset:
            pairs += [(i, i + step), (i + step, i)]
    return pairs


def split_bf16(x):
    high = x.astype(BF16)
    return high, (x - high.astype(F32)).astype(BF16)


def prep_kernel(meta_ref, toa_ref, dark_ref, near_ref, far_ref):
    half = toa_ref.shape[0] // 2
    even = meta_ref[0] == 0
    for field, band in ((0, 0), (1, 2)):
        lines = toa_ref[:, band, :].astype(F32) * dark_ref[...].astype(F32)
        lines = lines.astype(BF16)
        upper, lower = lines[:half], lines[half:]
        near_ref[field] = jnp.where(even, lower, upper)
        far_ref[field] = jnp.where(even, upper, lower)


def bands_kernel(taps_ref, rows_ref, cols_ref):
    taps = taps_ref[...]
    for out_ref, first in ((rows_ref, rows_ref.shape[1] // 2 - 30), (cols_ref, LANES - 30)):
        depth, width = out_ref.shape[1], out_ref.shape[2]
        base = taps
        if width > LANES:
            base = jnp.concatenate([taps, jnp.zeros((1, width - LANES), F32)], axis=1)
        base = jnp.broadcast_to(base, (8, width))
        base = pltpu.roll(base, 0, 1, stride=1, stride_axis=0)
        for at in range(0, depth, 16):
            pair = [pltpu.roll(base, first + at + 8 * k, 1) for k in range(2)]
            high, low = split_bf16(jnp.concatenate(pair, axis=0))
            out_ref[0, at : at + 16] = high
            out_ref[1, at : at + 16] = low


def vertical_kernel(meta_ref, bands_ref, near_ref, far_ref, near_in_ref, far_in_ref, out_ref, edge_ref):
    even = meta_ref[0] == 0
    left = meta_ref[1] == 0
    size = bands_ref.shape[1]
    matrix = jnp.concatenate([bands_ref[0], bands_ref[1]], axis=0)

    def field(index):
        near, far = near_ref[index], far_ref[index]
        near_in, far_in = near_in_ref[index], far_in_ref[index]
        return jnp.concatenate(
            [
                jnp.where(even, far_in, near_in),
                jnp.where(even, far, near),
                jnp.where(even, near, far),
                jnp.where(even, near_in, far_in),
            ],
            axis=0,
        )

    def along_rows(block):
        both = jnp.dot(matrix, block, preferred_element_type=F32)
        return both[:size] + both[size:]

    blue, red = field(0), field(1)
    dark = jnp.where(blue.astype(F32) > 0.0, 1.0, 0.0).astype(BF16)
    weighted = 8.0 * (along_rows(blue) - 0.5 * along_rows(red))
    darkness = along_rows(dark)
    for index, value in ((0, weighted), (1, darkness)):
        out_ref[index] = value
        edge_ref[index] = jnp.where(left, value[:, -LANES:], value[:, :LANES])


def correct_kernel(
    meta_ref,
    bands_ref,
    lut_ref,
    vert_ref,
    edge_ref,
    toa_ref,
    vapour_ref,
    class_ref,
    frac_ref,
    corr_ref,
    side0_ref,
    side1_ref,
    side2_ref,
    side3_ref,
    ext_ref,
    pos_ref,
    hat_ref,
    even_ref,
):
    rows, cols = vapour_ref.shape
    left = meta_ref[1] == 0
    levels_w = hat_ref.shape[0]
    levels_a = lut_ref.shape[1] // levels_w
    block = bands_ref.shape[1]
    window = bands_ref.shape[2]
    for index in range(2):
        edge = edge_ref[index]
        zero = jnp.zeros_like(edge)
        pieces = jnp.concatenate([jnp.where(left, zero, edge), vert_ref[index], jnp.where(left, edge, zero)], axis=1)
        high, low = split_bf16(pieces)
        ext_ref[index * rows : (index + 1) * rows, :] = high
        ext_ref[(2 + index) * rows : (3 + index) * rows, :] = low
    contract = (((1,), (1,)), ((), ()))
    for number in range(cols // block):
        at = slice(number * block, (number + 1) * block)
        part = ext_ref[:, number * block : number * block + window]
        full = lax.dot_general(part, bands_ref[0], contract, preferred_element_type=F32)
        rest = lax.dot_general(part[: 2 * rows], bands_ref[1], contract, preferred_element_type=F32)
        weighted = full[:rows] + full[2 * rows : 3 * rows] + rest[:rows]
        darkness = full[rows : 2 * rows] + full[3 * rows :] + rest[rows:]
        aerosol = weighted / jnp.maximum(darkness, 1.0)
        pos_ref[:, at] = (levels_a - 1.0) / (1.0 + jnp.exp(-aerosol))
    vapour = vapour_ref[...]
    for w in range(levels_w):
        hat_ref[w] = jnp.maximum(0.0, 1.0 - jnp.abs(vapour - float(w)))
    frac = frac_ref[...]
    even_ref[...] = jnp.where(class_ref[...] % 2 == 0, 1.0 - frac, frac)

    step = 256
    node_a = lax.broadcasted_iota(jnp.int32, (levels_a, step), 0).astype(F32)
    sublane = lax.broadcasted_iota(jnp.int32, (8, step), 0)
    upper = sublane >= 4
    shift = jnp.where(upper, 1, 0)
    lut = lut_ref[...]

    def row_step(row, carry):
        for number in range(cols // step):
            at = slice(number * step, (number + 1) * step)
            one = pl.ds(row, 1)
            pos = pos_ref[one, at]
            hat_a = jnp.maximum(0.0, 1.0 - jnp.abs(pos - node_a))
            joint = jnp.concatenate(
                [(hat_a * hat_ref[w, one, at]).astype(BF16) for w in range(levels_w)], axis=0
            )
            nodes = jnp.dot(lut, joint, preferred_element_type=F32)
            node = [nodes[8 * k : 8 * k + 8] for k in range(12)]
            level = jnp.broadcast_to(class_ref[one, at], (8, step))
            w_even = jnp.broadcast_to(even_ref[one, at], (8, step))
            w_odd = 1.0 - w_even
            even = jnp.where(level < 3, jnp.where(level < 1, node[0], node[2]), jnp.where(level < 5, node[4], node[6]))
            odd = jnp.where(level < 4, jnp.where(level < 2, node[1], node[3]), jnp.where(level < 6, node[5], node[7]))
            linear = w_even * even + w_odd * odd
            low = level - shift
            mixed = jnp.where(low < 3, jnp.where(low < 1, node[8], node[9]), jnp.where(low < 5, node[10], node[11]))
            mixed = mixed * jnp.where(upper, w_odd, w_even)
            albedo = mixed[:4] + mixed[4:]
            scaled = linear[:4] * toa_ref[row, :, at].astype(F32) - linear[4:]
            surface = scaled / (1.0 + albedo * scaled)
            corr_ref[row, :, at] = surface.astype(BF16)
        return carry

    lax.fori_loop(0, rows, row_step, 0)

    segments = rows // SEG
    band = lax.broadcasted_iota(jnp.int32, corr_ref.shape[1:], 0)
    for side, out_ref in enumerate((side0_ref, side1_ref, side2_ref, side3_ref)):
        target = meta_ref[2 + side]
        tags = jnp.zeros(corr_ref.shape[1:], F32)
        count = jnp.int32(0)
        for segment in range(segments):
            hit = meta_ref[6 + segment] == target
            slot = count

            @pl.when(hit)
            def _():
                out_ref[pl.ds(slot * SEG, SEG)] = corr_ref[segment * SEG : (segment + 1) * SEG]

            tag = jnp.where(hit, meta_ref[6 + 2 * segments + segment] + 1, 0).astype(F32)
            tags = tags + jnp.where(band == slot, tag, 0.0)
            count = count + hit.astype(jnp.int32)
        out_ref[CAP * SEG] = tags.astype(BF16)


def own_kernel(meta_ref, corr_ref, acc_ref):
    rows = corr_ref.shape[0]
    segments = rows // SEG
    acc_ref[...] = jnp.zeros(acc_ref.shape, F32)
    for segment in range(segments):
        start = meta_ref[6 + segments + segment]
        at = pl.ds(start, SEG)
        acc_ref[at] = acc_ref[at] + corr_ref[segment * SEG : (segment + 1) * SEG].astype(F32)


def combine_kernel(meta_ref, acc_in_ref, side0_ref, side1_ref, side2_ref, side3_ref, out_ref, acc_ref, inv_ref):
    rows = acc_ref.shape[0]
    segments = rows // SEG
    line = lax.broadcasted_iota(jnp.int32, (rows, LANES), 0)

    def covers(start):
        return jnp.where((line >= start) & (line < start + SEG), 1.0, 0.0)

    count = jnp.zeros((rows, LANES), F32)
    for segment in range(segments):
        count = count + covers(meta_ref[6 + segments + segment])
    acc_ref[...] = acc_in_ref[...]
    for side_ref in (side0_ref, side1_ref, side2_ref, side3_ref):
        tags = side_ref[CAP * SEG, :, :LANES].astype(F32)
        band = lax.broadcasted_iota(jnp.int32, tags.shape, 0)
        for slot in range(CAP):
            tag = jnp.max(jnp.where(band == slot, tags, 0.0)).astype(jnp.int32)
            start = jnp.maximum(tag - 1, 0)
            count = count + jnp.where(tag > 0, covers(start), 0.0)

            @pl.when(tag > 0)
            def _():
                at = pl.ds(start, SEG)
                acc_ref[at] = acc_ref[at] + side_ref[slot * SEG : (slot + 1) * SEG].astype(F32)

    inv_ref[...] = 1.0 / jnp.maximum(count, 1.0)
    repeat = out_ref.shape[2] // LANES
    for row in range(rows):
        inverse = jnp.broadcast_to(inv_ref[row : row + 1, :], (out_ref.shape[1], LANES))
        inverse = jnp.concatenate([inverse] * repeat, axis=1)
        out_ref[row] = (acc_ref[row] * inverse).astype(BF16)


def body(
    toa_bands,
    dark_mask,
    vapour,
    elev_class,
    elev_frac,
    kernel,
    lut_gain,
    lut_path,
    lut_albedo,
    routes,
    starts,
):
    rows, bands, cols = toa_bands.shape
    levels_e, levels_a, levels_w = lut_gain.shape[1:]
    nodes = levels_a * levels_w
    count = lax.axis_size("along")
    me = lax.axis_index("along")
    core = lax.axis_index("across")
    near = 1 - 2 * (me % 2)
    far_z = 2 - 4 * ((me // 2) % 2)
    distance = routes[:, 1] - me
    meta = jnp.concatenate(
        [jnp.stack([me % 2, core, near, -near, far_z, -far_z]), distance, starts[:, 0], starts[:, 1]]
    ).astype(jnp.int32)
    half = rows // 2
    fields = jax.ShapeDtypeStruct((2, half, cols), BF16)
    near_out, far_out = pl.pallas_call(
        prep_kernel,
        out_shape=(fields, fields),
        in_specs=[SMEM, VMEM, VMEM],
        out_specs=(VMEM, VMEM),
        compiler_params=params(),
        name="prep",
    )(meta, toa_bands, dark_mask)
    near_in = lax.ppermute(near_out, "along", swap_pairs(count, 1, 0))
    far_in = lax.ppermute(far_out, "along", swap_pairs(count, 1, 1))
    taps = jnp.pad(kernel, (0, LANES - kernel.shape[0]))[None, :]
    block = 256
    row_bands, col_bands = pl.pallas_call(
        bands_kernel,
        out_shape=(
            jax.ShapeDtypeStruct((2, rows, 2 * rows), BF16),
            jax.ShapeDtypeStruct((2, block, block + 2 * LANES), BF16),
        ),
        in_specs=[VMEM],
        out_specs=(VMEM, VMEM),
        compiler_params=params(),
        name="bands",
    )(taps)
    lut_first = jnp.concatenate([lut_gain, lut_path], axis=0).transpose(1, 0, 3, 2)
    lut_last = lut_albedo.transpose(1, 0, 3, 2)
    lut = jnp.concatenate(
        [lut_first.reshape(2 * bands * levels_e, nodes), lut_last.reshape(bands * levels_e, nodes)], axis=0
    )
    vert, edge = pl.pallas_call(
        vertical_kernel,
        out_shape=(
            jax.ShapeDtypeStruct((2, rows, cols), F32),
            jax.ShapeDtypeStruct((2, rows, LANES), F32),
        ),
        in_specs=[SMEM] + [VMEM] * 5,
        out_specs=(VMEM, VMEM),
        compiler_params=params(),
        name="vertical",
    )(meta, row_bands, near_out, far_out, near_in, far_in)
    edge_in = lax.ppermute(edge, "across", swap_pairs(lax.axis_size("across"), 1, 0))
    slots = jax.ShapeDtypeStruct((CAP * SEG + 1, bands, cols), BF16)
    corr, *sides = pl.pallas_call(
        correct_kernel,
        out_shape=(jax.ShapeDtypeStruct((rows, bands, cols), BF16),) + (slots,) * 4,
        in_specs=[SMEM] + [VMEM] * 8,
        out_specs=(VMEM,) * 5,
        scratch_shapes=[
            pltpu.VMEM((4 * rows, cols + 2 * LANES), BF16),
            pltpu.VMEM((rows, cols), F32),
            pltpu.VMEM((levels_w, rows, cols), F32),
            pltpu.VMEM((rows, cols), F32),
        ],
        compiler_params=params(),
        name="correct",
    )(meta, col_bands, lut, vert, edge_in, toa_bands, vapour, elev_class, elev_frac)
    moves = ((1, 0), (1, 1), (2, 0), (2, 1))
    got = [
        lax.ppermute(side, "along", swap_pairs(count, step, offset)) for side, (step, offset) in zip(sides, moves)
    ]
    total = jax.ShapeDtypeStruct((rows, bands, cols), F32)
    acc = pl.pallas_call(
        own_kernel,
        out_shape=total,
        in_specs=[SMEM, VMEM],
        out_specs=VMEM,
        compiler_params=params(),
        name="own",
    )(meta, corr)
    out = pl.pallas_call(
        combine_kernel,
        out_shape=jax.ShapeDtypeStruct((rows, bands, cols), BF16),
        in_specs=[SMEM] + [VMEM] * 5,
        out_specs=VMEM,
        scratch_shapes=[pltpu.VMEM((rows, bands, cols), F32), pltpu.VMEM((rows, LANES), F32)],
        compiler_params=params(),
        name="combine",
    )(meta, acc, *got)
    return out[None]


def solution(mesh):
    in_specs = (
        P(("groups", "along"), None, "across"),
        P(("groups", "along"), "across"),
        P(("groups", "along"), "across"),
        P(("groups", "along"), "across"),
        P(("groups", "along"), "across"),
        P(),
        P(),
        P(),
        P(),
        P(("groups", "along"), None),
        P(("groups", "along"), None),
    )
    out_specs = P(("groups", "along"), None, None, "across")
    return jax.shard_map(body, mesh=mesh, in_specs=in_specs, out_specs=out_specs, check_vma=False)
```

```python
import functools

import jax
import jax.numpy as jnp
from jax import lax
from jax.experimental import pallas as pl
from jax.experimental.pallas import tpu as pltpu
from jax.sharding import PartitionSpec as P

SEG = 16
CAP = 2
LANES = 128

F32 = jnp.float32
BF16 = jnp.bfloat16
VMEM = pl.BlockSpec(memory_space=pltpu.VMEM)
HBM = pl.BlockSpec(memory_space=pltpu.HBM)
SMEM = pl.BlockSpec(memory_space=pltpu.SMEM)


def params(mib=32):
    return pltpu.CompilerParams(vmem_limit_bytes=mib * 1024 * 1024)


def swap_pairs(count, step, offset):
    pairs = []
    for i in range(count - step):
        if (i // step) % 2 == offset:
            pairs += [(i, i + step), (i + step, i)]
    return pairs


def split_bf16(x):
    high = x.astype(BF16)
    return high, (x - high.astype(F32)).astype(BF16)


def prep_kernel(toa_ref, dark_ref, near_ref, far_ref, toa_in, dark_in, sems):
    rows = toa_in.shape[0]
    parts = 4
    size = rows // parts
    even = lax.axis_index("along") % 2 == 0
    copies = []
    for part in range(parts):
        at = pl.ds(part * size, size)
        copies.append(
            (
                pltpu.make_async_copy(toa_ref.at[at], toa_in.at[at], sems.at[0, part]),
                pltpu.make_async_copy(dark_ref.at[at], dark_in.at[at], sems.at[1, part]),
            )
        )
        for copy in copies[-1]:
            copy.start()
    for part in range(parts):
        for copy in copies[part]:
            copy.wait()
        at = slice(part * size, (part + 1) * size)
        to = slice(part % 2 * size, (part % 2 + 1) * size)
        into_near = even if part >= 2 else jnp.logical_not(even)
        dark = dark_in[at].astype(F32)
        lines = [(toa_in[at, band, :].astype(F32) * dark).astype(BF16) for band in (0, 2)]
        for flag, out_ref in ((into_near, near_ref), (jnp.logical_not(into_near), far_ref)):

            @pl.when(flag)
            def _():
                for field in range(2):
                    out_ref[field, to] = lines[field]


def bands_kernel(taps_ref, rows_ref, cols_ref):
    taps = taps_ref[...]
    for out_ref, first in ((rows_ref, rows_ref.shape[1] - 30), (cols_ref, LANES - 30)):
        depth, width = out_ref.shape[1], out_ref.shape[2]
        base = taps
        if width > LANES:
            base = jnp.concatenate([taps, jnp.zeros((1, width - LANES), F32)], axis=1)
        base = jnp.broadcast_to(base, (8, base.shape[1]))
        base = pltpu.roll(base, 0, 1, stride=1, stride_axis=0)
        for at in range(0, depth, 16):
            pair = [pltpu.roll(base, first + at + 8 * k, 1)[:, :width] for k in range(2)]
            high, low = split_bf16(jnp.concatenate(pair, axis=0))
            out_ref[0, at : at + 16] = high
            out_ref[1, at : at + 16] = low


def is_half(flip):
    return lax.axis_index("along") % 2 == flip


def vertical_kernel(flip, bands_ref, here_ref, beside_ref, in_ref, *rest):
    ext_ref, edge_ref = rest[-2:]
    lower = is_half(flip)
    left = lax.axis_index("across") == 0
    size = bands_ref.shape[1]
    matrix = jnp.concatenate([bands_ref[0], bands_ref[1]], axis=0)

    def field(index):
        beside, incoming = beside_ref[index], in_ref[index]
        return jnp.concatenate(
            [jnp.where(lower, beside, incoming), here_ref[index], jnp.where(lower, incoming, beside)], axis=0
        )

    def smooth(block):
        both = jnp.dot(matrix, block, preferred_element_type=F32)
        return both[:size] + both[size:]

    blue, red = field(0), field(1)
    dark = jnp.where(blue.astype(F32) > 0.0, 1.0, 0.0).astype(BF16)
    for index, value in enumerate((8.0 * (smooth(blue) - 0.5 * smooth(red)), smooth(dark))):
        edge_ref[index] = jnp.where(left, value[:, -LANES:], value[:, :LANES])
        high, low = split_bf16(value)
        ext_ref[0, index] = high
        ext_ref[1, index] = low


def hats_kernel(vapour_ref, class_ref, frac_ref, *halves):
    for flip in range(2):
        hat_ref, even_ref = halves[2 * flip : 2 * flip + 2]
        rows = even_ref.shape[0]
        here = pl.ds(pl.multiple_of(jnp.where(is_half(flip), rows, 0), rows), rows)
        vapour = vapour_ref[here]
        for w in range(hat_ref.shape[0]):
            hat_ref[w] = jnp.maximum(0.0, 1.0 - jnp.abs(vapour - float(w)))
        frac = frac_ref[here]
        even_ref[...] = jnp.where(class_ref[here] % 2 == 0, 1.0 - frac, frac)


def correct_rows(
    flip,
    bands_ref,
    lut_ref,
    edge_ref,
    ext_ref,
    hat_ref,
    even_ref,
    toa_ref,
    class_ref,
    corr_ref,
    pos_ref,
):
    rows, cols = pos_ref.shape
    base = pl.multiple_of(jnp.where(is_half(flip), rows, 0), rows)
    left = lax.axis_index("across") == 0
    levels_w = hat_ref.shape[0]
    levels_a = lut_ref.shape[1] // (2 * levels_w)
    block = bands_ref.shape[1]
    window = bands_ref.shape[2]
    lines = []
    for index in range(2):
        terms = split_bf16(edge_ref[index])
        for k in range(2):
            none = jnp.zeros_like(terms[k])
            lines.append((jnp.where(left, none, terms[k]), ext_ref[k, index], jnp.where(left, terms[k], none)))
    lines = [jnp.concatenate(line, axis=1) for line in (lines[0], lines[2], lines[1], lines[3])]
    windows = [slice(number * block, number * block + window) for number in range(cols // block)]
    contract = (((1,), (1,)), ((), ()))
    every = jnp.concatenate([line[:, at] for line in lines for at in windows], axis=0)
    full = lax.dot_general(every, bands_ref[0], contract, preferred_element_type=F32)
    rest = lax.dot_general(every[: every.shape[0] // 2], bands_ref[1], contract, preferred_element_type=F32)
    pieces = len(windows)
    for number in range(pieces):
        at = slice(number * block, (number + 1) * block)

        def part(array, line):
            return array[(line * pieces + number) * rows : (line * pieces + number + 1) * rows]

        weighted = part(full, 0) + (part(full, 2) + part(rest, 0))
        darkness = part(full, 1) + (part(full, 3) + part(rest, 1))
        aerosol = weighted / jnp.maximum(darkness, 1.0)
        pos_ref[:, at] = (levels_a - 1.0) / (1.0 + jnp.exp(-aerosol))

    step = 256
    node_a = lax.broadcasted_iota(jnp.int32, (levels_a, step), 0).astype(F32)
    second = lax.broadcasted_iota(jnp.int32, (8, step), 0) >= 4
    lut = lut_ref[...]

    def pair(row, number):
        at = slice(number * step, (number + 1) * step)
        pieces = []
        for k in range(2):
            one = pl.ds(row + k, 1)
            hat_a = jnp.maximum(0.0, 1.0 - jnp.abs(pos_ref[one, at] - node_a)).astype(BF16)
            pieces += [
                hat_a * jnp.broadcast_to(hat_ref[w, one, at], (levels_a, step)).astype(BF16) for w in range(levels_w)
            ]
        nodes = jnp.dot(lut, jnp.concatenate(pieces, axis=0), preferred_element_type=F32)

        def both(ref, first):
            one, two = (jnp.broadcast_to(ref[pl.ds(first + k, 1), at], (8, step)) for k in range(2))
            return jnp.where(second, two, one)

        level = both(class_ref, base + row)
        w_even = both(even_ref, row)
        w_odd = 1.0 - w_even
        below = [level < k for k in range(7)]

        def coefficient(table):
            node = [nodes[64 * table + 8 * k : 64 * table + 8 * k + 8] for k in range(8)]
            even = jnp.where(
                below[3], jnp.where(below[1], node[0], node[2]), jnp.where(below[5], node[4], node[6])
            )
            odd = jnp.where(
                below[4], jnp.where(below[2], node[1], node[3]), jnp.where(below[6], node[5], node[7])
            )
            return w_even * even + w_odd * odd

        toa = jnp.concatenate([toa_ref[base + row + k, :, at].astype(F32) for k in range(2)], axis=0)
        scaled = coefficient(0) * toa - coefficient(1)
        surface = scaled / (1.0 + coefficient(2) * scaled)
        corr_ref[row, :, at] = surface[:4].astype(BF16)
        corr_ref[row + 1, :, at] = surface[4:].astype(BF16)

    group = 16

    def group_step(number, carry):
        for k in range(0, group, 2):
            for piece in range(cols // step):
                pair(number * group + k, piece)
        return carry

    lax.fori_loop(0, rows // group, group_step, 0)


def correct_near_kernel(*refs):
    correct_rows(0, *refs)


def segment_list(near_ref, far_ref):
    each = far_ref.shape[0] // SEG
    shift = jnp.where(is_half(0), each, 0)
    return [(shift + k, near_ref, k) for k in range(each)] + [(each - shift + k, far_ref, k) for k in range(each)]


def correct_far_kernel(meta_ref, *refs):
    near_ref, corr_ref, sides = refs[8], refs[9], refs[10:14]
    correct_rows(1, *refs[:8], corr_ref, *refs[14:])
    listed = segment_list(near_ref, corr_ref)
    segments = len(listed)
    band = lax.broadcasted_iota(jnp.int32, corr_ref.shape[1:], 0)
    for side, out_ref in enumerate(sides):
        target = meta_ref[side]
        tags = jnp.zeros(corr_ref.shape[1:], F32)
        count = jnp.int32(0)
        for segment, from_ref, place in listed:
            hit = meta_ref[4 + segment] == target
            slot = count

            @pl.when(hit)
            def _():
                out_ref[pl.ds(slot * SEG, SEG)] = from_ref[place * SEG : (place + 1) * SEG]

            tag = jnp.where(hit, meta_ref[4 + 2 * segments + segment] + 1, 0).astype(F32)
            tags = tags + jnp.where(band == slot, tag, 0.0)
            count = count + hit.astype(jnp.int32)
        out_ref[CAP * SEG] = tags.astype(BF16)


def add_rows(acc_ref, start, from_ref, place):
    for row in range(SEG):
        acc_ref[start + row] = acc_ref[start + row] + from_ref[place * SEG + row].astype(F32)


def covers(rows, start):
    line = lax.broadcasted_iota(jnp.int32, (rows, LANES), 0)
    return jnp.where((line >= start) & (line < start + SEG), 1.0, 0.0)


def read_tags(side_refs):
    found = []
    for side_ref in side_refs:
        tags = side_ref[CAP * SEG, :, :LANES].astype(F32)
        band = lax.broadcasted_iota(jnp.int32, tags.shape, 0)
        for slot in range(CAP):
            found.append((jnp.max(jnp.where(band == slot, tags, 0.0)).astype(jnp.int32), side_ref, slot))
    return found


def add_sides(acc_ref, count, side_refs):
    found = read_tags(side_refs)
    for tag, side_ref, slot in found:
        start = jnp.maximum(tag - 1, 0)
        count = count + jnp.where(tag > 0, covers(count.shape[0], start), 0.0)

        @pl.when(tag > 0)
        def _():
            add_rows(acc_ref, start, side_ref, slot)

    return count


def own_kernel(meta_ref, near_ref, far_ref, acc_ref, count_ref):
    acc_ref[...] = jnp.zeros(acc_ref.shape, F32)
    count = jnp.zeros(count_ref.shape, F32)
    listed = segment_list(near_ref, far_ref)
    for segment, from_ref, place in listed:
        start = meta_ref[4 + len(listed) + segment]
        count = count + covers(count.shape[0], start)
        add_rows(acc_ref, start, from_ref, place)
    count_ref[...] = count


def add_kernel(acc_in_ref, count_in_ref, side0_ref, side1_ref, acc_ref, count_ref):
    count_ref[...] = add_sides(acc_ref, count_in_ref[...], (side0_ref, side1_ref))


def last_kernel(acc_in_ref, count_in_ref, side0_ref, side1_ref, acc_ref, out_ref, inv_ref):
    count = add_sides(acc_ref, count_in_ref[...], (side0_ref, side1_ref))
    inv_ref[...] = 1.0 / jnp.maximum(count, 1.0)
    repeat = out_ref.shape[2] // LANES
    for row in range(out_ref.shape[0]):
        inverse = jnp.broadcast_to(inv_ref[row : row + 1, :], (out_ref.shape[1], LANES))
        inverse = jnp.concatenate([inverse] * repeat, axis=1)
        out_ref[row] = (acc_ref[row] * inverse).astype(BF16)


def body(
    toa_bands,
    dark_mask,
    vapour,
    elev_class,
    elev_frac,
    kernel,
    lut_gain,
    lut_path,
    lut_albedo,
    routes,
    starts,
):
    rows, bands, cols = toa_bands.shape
    levels_e, levels_a, levels_w = lut_gain.shape[1:]
    nodes = levels_a * levels_w
    count = lax.axis_size("along")
    me = lax.axis_index("along")
    near = 1 - 2 * (me % 2)
    far_z = 2 - 4 * ((me // 2) % 2)
    distance = routes[:, 1] - me
    meta = jnp.concatenate(
        [jnp.stack([near, -near, far_z, -far_z]), distance, starts[:, 0], starts[:, 1]]
    ).astype(jnp.int32)
    half = rows // 2
    fields = jax.ShapeDtypeStruct((2, half, cols), BF16)
    near_out, far_out = pl.pallas_call(
        prep_kernel,
        out_shape=(fields, fields),
        in_specs=[HBM, HBM],
        out_specs=(VMEM, VMEM),
        scratch_shapes=[
            pltpu.VMEM((rows, bands, cols), BF16),
            pltpu.VMEM((rows, cols), jnp.int32),
            pltpu.SemaphoreType.DMA((2, 4)),
        ],
        compiler_params=params(62),
        name="prep",
    )(toa_bands, dark_mask)
    near_in = lax.ppermute(near_out, "along", swap_pairs(count, 1, 0))
    far_in = lax.ppermute(far_out, "along", swap_pairs(count, 1, 1))
    taps = jnp.pad(kernel, (0, LANES - kernel.shape[0]))[None, :]
    block = 256
    row_bands, col_bands = pl.pallas_call(
        bands_kernel,
        out_shape=(
            jax.ShapeDtypeStruct((2, half, 3 * half), BF16),
            jax.ShapeDtypeStruct((2, block, block + 2 * LANES), BF16),
        ),
        in_specs=[VMEM],
        out_specs=(VMEM, VMEM),
        compiler_params=params(),
        name="bands",
    )(taps)
    tables = jnp.stack([lut_gain, lut_path, lut_albedo]).transpose(0, 2, 1, 4, 3)
    tables = tables.reshape(3, levels_e, bands, nodes)
    blank = jnp.zeros_like(tables)
    lut = jnp.stack(
        [jnp.concatenate([tables, blank], axis=3), jnp.concatenate([blank, tables], axis=3)], axis=2
    ).reshape(6 * levels_e * bands, 2 * nodes)

    def smooth_rows(flip, here, beside, incoming, *after):
        ext, edge = pl.pallas_call(
            functools.partial(vertical_kernel, flip),
            out_shape=(
                jax.ShapeDtypeStruct((2, 2, half, cols), BF16),
                jax.ShapeDtypeStruct((2, half, LANES), F32),
            ),
            in_specs=[VMEM] * (4 + len(after)),
            out_specs=(VMEM, VMEM),
            compiler_params=params(),
            name="vertical",
        )(row_bands, here, beside, incoming, *after)
        return lax.ppermute(edge, "across", swap_pairs(lax.axis_size("across"), 1, 0)), ext

    weights = (
        jax.ShapeDtypeStruct((levels_w, half, cols), F32),
        jax.ShapeDtypeStruct((half, cols), F32),
    )
    near_hats, near_even, far_hats, far_even = pl.pallas_call(
        hats_kernel,
        out_shape=weights * 2,
        in_specs=[VMEM] * 3,
        out_specs=(VMEM,) * 4,
        compiler_params=params(),
        name="hats",
    )(vapour, elev_class, elev_frac)
    corrected = jax.ShapeDtypeStruct((half, bands, cols), BF16)
    scratch = [pltpu.VMEM((half, cols), F32)]
    near_corr = pl.pallas_call(
        correct_near_kernel,
        out_shape=corrected,
        in_specs=[VMEM] * 8,
        out_specs=VMEM,
        scratch_shapes=scratch,
        compiler_params=params(),
        name="correct_near",
    )(col_bands, lut, *smooth_rows(0, near_out, far_out, near_in), near_hats, near_even, toa_bands, elev_class)
    far_edge, far_ext = smooth_rows(1, far_out, near_out, far_in, near_corr)
    slots = jax.ShapeDtypeStruct((CAP * SEG + 1, bands, cols), BF16)
    far_corr, *sides = pl.pallas_call(
        correct_far_kernel,
        out_shape=(corrected,) + (slots,) * 4,
        in_specs=[SMEM] + [VMEM] * 9,
        out_specs=(VMEM,) * 5,
        scratch_shapes=scratch,
        compiler_params=params(),
        name="correct_far",
    )(meta, col_bands, lut, far_edge, far_ext, far_hats, far_even, toa_bands, elev_class, near_corr)
    moves = ((1, 0), (1, 1), (2, 0), (2, 1))
    got = [
        lax.ppermute(side, "along", swap_pairs(count, step, offset)) for side, (step, offset) in zip(sides, moves)
    ]
    total = jax.ShapeDtypeStruct((rows, bands, cols), F32)
    counts = jax.ShapeDtypeStruct((rows, LANES), F32)
    acc, number = pl.pallas_call(
        own_kernel,
        out_shape=(total, counts),
        in_specs=[SMEM, VMEM, VMEM],
        out_specs=(VMEM, VMEM),
        compiler_params=params(),
        name="own",
    )(meta, near_corr, far_corr)
    acc, number = pl.pallas_call(
        add_kernel,
        out_shape=(total, counts),
        in_specs=[VMEM] * 4,
        out_specs=(VMEM, VMEM),
        input_output_aliases={0: 0, 1: 1},
        compiler_params=params(),
        name="add",
    )(acc, number, got[0], got[1])
    _, out = pl.pallas_call(
        last_kernel,
        out_shape=(total, jax.ShapeDtypeStruct((rows, bands, cols), BF16)),
        in_specs=[VMEM] * 4,
        out_specs=(VMEM, VMEM),
        scratch_shapes=[pltpu.VMEM((rows, LANES), F32)],
        input_output_aliases={0: 0},
        compiler_params=params(),
        name="last",
    )(acc, number, got[2], got[3])
    return out[None]


def solution(mesh):
    in_specs = (
        P(("groups", "along"), None, "across"),
        P(("groups", "along"), "across"),
        P(("groups", "along"), "across"),
        P(("groups", "along"), "across"),
        P(("groups", "along"), "across"),
        P(),
        P(),
        P(),
        P(),
        P(("groups", "along"), None),
        P(("groups", "along"), None),
    )
    out_specs = P(("groups", "along"), None, None, "across")
    return jax.shard_map(body, mesh=mesh, in_specs=in_specs, out_specs=out_specs, check_vma=False)
```

```python
import functools

import jax
import jax.numpy as jnp
from jax import lax
from jax.experimental import pallas as pl
from jax.experimental.pallas import tpu as pltpu
from jax.sharding import PartitionSpec as P

SEG = 16
CAP = 2
LANES = 128

F32 = jnp.float32
BF16 = jnp.bfloat16
VMEM = pl.BlockSpec(memory_space=pltpu.VMEM)
HBM = pl.BlockSpec(memory_space=pltpu.HBM)
SMEM = pl.BlockSpec(memory_space=pltpu.SMEM)


def params(mib=24):
    return pltpu.CompilerParams(vmem_limit_bytes=mib * 1024 * 1024)


def swap_pairs(count, step, offset):
    pairs = []
    for i in range(count - step):
        if (i // step) % 2 == offset:
            pairs += [(i, i + step), (i + step, i)]
    return pairs


def in_hbm(*arrays):
    return [pltpu.with_memory_space_constraint(array, pltpu.HBM) for array in arrays]


def split_bf16(x):
    high = x.astype(BF16)
    return high, (x - high.astype(F32)).astype(BF16)


def prep_kernel(toa_ref, dark_ref, near_ref, far_ref, toa_in, dark_in, sems):
    rows = toa_in.shape[0]
    parts = 4
    size = rows // parts
    even = lax.axis_index("along") % 2 == 0
    copies = []
    for part in range(parts):
        at = pl.ds(part * size, size)
        copies.append(
            (
                pltpu.make_async_copy(toa_ref.at[at], toa_in.at[at], sems.at[0, part]),
                pltpu.make_async_copy(dark_ref.at[at], dark_in.at[at], sems.at[1, part]),
            )
        )
        for copy in copies[-1]:
            copy.start()
    for part in range(parts):
        for copy in copies[part]:
            copy.wait()
        at = slice(part * size, (part + 1) * size)
        to = slice(part % 2 * size, (part % 2 + 1) * size)
        into_near = even if part >= 2 else jnp.logical_not(even)
        dark = dark_in[at].astype(F32)
        lines = [(toa_in[at, band, :].astype(F32) * dark).astype(BF16) for band in (0, 2)]
        for flag, out_ref in ((into_near, near_ref), (jnp.logical_not(into_near), far_ref)):

            @pl.when(flag)
            def _():
                for field in range(2):
                    out_ref[field, to] = lines[field]


def store_bands(taps, out_ref, first):
    depth, width = out_ref.shape[1], out_ref.shape[2]
    base = taps
    if width > LANES:
        base = jnp.concatenate([taps, jnp.zeros((1, width - LANES), F32)], axis=1)
    base = jnp.broadcast_to(base, (8, base.shape[1]))
    base = pltpu.roll(base, 0, 1, stride=1, stride_axis=0)
    for at in range(0, depth, 16):
        pair = [pltpu.roll(base, first + at + 8 * k, 1)[:, :width] for k in range(2)]
        high, low = split_bf16(jnp.concatenate(pair, axis=0))
        out_ref[0, at : at + 16] = high
        out_ref[1, at : at + 16] = low


def is_half(flip):
    return lax.axis_index("along") % 2 == flip


def vertical_kernel(flip, bands_ref, here_ref, beside_ref, in_ref, *rest):
    ext_ref, edge_ref = rest[-2:]
    lower = is_half(flip)
    left = lax.axis_index("across") == 0
    size = bands_ref.shape[1]
    matrix = jnp.concatenate([bands_ref[0], bands_ref[1]], axis=0)

    def field(index):
        beside, incoming = beside_ref[index], in_ref[index]
        return jnp.concatenate(
            [jnp.where(lower, beside, incoming), here_ref[index], jnp.where(lower, incoming, beside)], axis=0
        )

    def smooth(block):
        both = jnp.dot(matrix, block, preferred_element_type=F32)
        return both[:size] + both[size:]

    blue, red = field(0), field(1)
    dark = jnp.where(blue.astype(F32) > 0.0, 1.0, 0.0).astype(BF16)
    for index, value in enumerate((8.0 * (smooth(blue) - 0.5 * smooth(red)), smooth(dark))):
        edge_ref[index] = jnp.where(left, value[:, -LANES:], value[:, :LANES])
        high, low = split_bf16(value)
        ext_ref[0, index] = high
        ext_ref[1, index] = low


def store_table(array, out_ref, table, shape):
    bands, levels_e, levels_w, levels_a = shape
    nodes = levels_w * levels_a

    def iota(size, dim):
        return lax.broadcasted_iota(jnp.int32, size, dim)

    repeat = iota((levels_a, nodes), 1) % levels_a == iota((levels_a, nodes), 0)
    spread = jnp.dot(array, jnp.where(repeat, 1.0, 0.0).astype(BF16), preferred_element_type=F32)
    own = iota(spread.shape, 1) // levels_a == iota(spread.shape, 0) % levels_w
    spread = jnp.where(own, spread, 0.0).astype(BF16)
    size = (2 * bands * levels_e, spread.shape[0])
    row, source = iota(size, 0), iota(size, 1) // levels_w
    wanted = row % bands * levels_e + row // (2 * bands)
    for k in range(2):
        pick = (source == wanted) & (row // bands % 2 == k)
        part = jnp.dot(jnp.where(pick, 1.0, 0.0).astype(BF16), spread, preferred_element_type=F32)
        out_ref[table * size[0] : (table + 1) * size[0], k * nodes : (k + 1) * nodes] = part.astype(BF16)


def early_kernel(
    shape,
    gain_ref,
    path_ref,
    albedo_ref,
    taps_ref,
    vapour_ref,
    class_ref,
    frac_ref,
    lut_ref,
    rows_ref,
    cols_ref,
    vapour_out_ref,
    class_out_ref,
    frac_out_ref,
    tables_in,
    taps_in,
    sems,
):
    tables = [(source, tables_in.at[k]) for k, source in enumerate((gain_ref, path_ref, albedo_ref))]
    others = [(vapour_ref, vapour_out_ref), (class_ref, class_out_ref), (frac_ref, frac_out_ref)]
    pairs = [(taps_ref, taps_in)] + tables + others
    copies = [pltpu.make_async_copy(source, into, sems.at[k]) for k, (source, into) in enumerate(pairs)]
    for copy in copies:
        copy.start()
    copies[0].wait()
    taps = taps_in[...]
    taps = jnp.concatenate([taps, jnp.zeros((1, LANES - taps.shape[1]), F32)], axis=1)
    store_bands(taps, rows_ref, rows_ref.shape[1] - 30)
    store_bands(taps, cols_ref, LANES - 30)
    for table in range(3):
        copies[1 + table].wait()
        store_table(tables_in[table], lut_ref, table, shape)
    for copy in copies[4:]:
        copy.wait()


def hats_kernel(flip, vapour_ref, class_ref, frac_ref, *rest):
    hat_ref, even_ref = rest[-2:]
    rows = even_ref.shape[0]
    here = pl.ds(pl.multiple_of(jnp.where(is_half(flip), rows, 0), rows), rows)
    vapour = vapour_ref[here]
    for w in range(hat_ref.shape[0]):
        hat_ref[w] = jnp.maximum(0.0, 1.0 - jnp.abs(vapour - float(w)))
    frac = frac_ref[here]
    even_ref[...] = jnp.where(class_ref[here] % 2 == 0, 1.0 - frac, frac)


def correct_rows(
    flip,
    bands_ref,
    lut_ref,
    edge_ref,
    ext_ref,
    hat_ref,
    even_ref,
    toa_ref,
    class_ref,
    corr_ref,
    pos_ref,
):
    rows, cols = pos_ref.shape
    base = pl.multiple_of(jnp.where(is_half(flip), rows, 0), rows)
    left = lax.axis_index("across") == 0
    levels_w = hat_ref.shape[0]
    levels_a = lut_ref.shape[1] // (2 * levels_w)
    block = bands_ref.shape[1]
    window = bands_ref.shape[2]
    lines = []
    for index in range(2):
        terms = split_bf16(edge_ref[index])
        for k in range(2):
            none = jnp.zeros_like(terms[k])
            lines.append((jnp.where(left, none, terms[k]), ext_ref[k, index], jnp.where(left, terms[k], none)))
    lines = [jnp.concatenate(line, axis=1) for line in (lines[0], lines[2], lines[1], lines[3])]
    windows = [slice(number * block, number * block + window) for number in range(cols // block)]
    contract = (((1,), (1,)), ((), ()))
    every = jnp.concatenate([line[:, at] for line in lines for at in windows], axis=0)
    full = lax.dot_general(every, bands_ref[0], contract, preferred_element_type=F32)
    rest = lax.dot_general(every[: every.shape[0] // 2], bands_ref[1], contract, preferred_element_type=F32)
    pieces = len(windows)
    for number in range(pieces):
        at = slice(number * block, (number + 1) * block)

        def part(array, line):
            return array[(line * pieces + number) * rows : (line * pieces + number + 1) * rows]

        weighted = part(full, 0) + (part(full, 2) + part(rest, 0))
        darkness = part(full, 1) + (part(full, 3) + part(rest, 1))
        aerosol = weighted / jnp.maximum(darkness, 1.0)
        pos_ref[:, at] = (levels_a - 1.0) / (1.0 + jnp.exp(-aerosol))

    step = 256
    node_a = lax.broadcasted_iota(jnp.int32, (levels_a, step), 0).astype(F32)
    second = lax.broadcasted_iota(jnp.int32, (8, step), 0) >= 4
    lut = lut_ref[...]

    def pair(row, number):
        at = slice(number * step, (number + 1) * step)
        pieces = []
        for k in range(2):
            one = pl.ds(row + k, 1)
            hat_a = jnp.maximum(0.0, 1.0 - jnp.abs(pos_ref[one, at] - node_a)).astype(BF16)
            pieces += [
                hat_a * jnp.broadcast_to(hat_ref[w, one, at], (levels_a, step)).astype(BF16) for w in range(levels_w)
            ]
        nodes = jnp.dot(lut, jnp.concatenate(pieces, axis=0), preferred_element_type=F32)

        def both(ref, first):
            one, two = (jnp.broadcast_to(ref[pl.ds(first + k, 1), at], (8, step)) for k in range(2))
            return jnp.where(second, two, one)

        level = both(class_ref, base + row)
        w_even = both(even_ref, row)
        w_odd = 1.0 - w_even
        below = [level < k for k in range(7)]

        def coefficient(table):
            node = [nodes[64 * table + 8 * k : 64 * table + 8 * k + 8] for k in range(8)]
            even = jnp.where(
                below[3], jnp.where(below[1], node[0], node[2]), jnp.where(below[5], node[4], node[6])
            )
            odd = jnp.where(
                below[4], jnp.where(below[2], node[1], node[3]), jnp.where(below[6], node[5], node[7])
            )
            return w_even * even + w_odd * odd

        toa = jnp.concatenate([toa_ref[base + row + k, :, at].astype(F32) for k in range(2)], axis=0)
        scaled = coefficient(0) * toa - coefficient(1)
        surface = scaled / (1.0 + coefficient(2) * scaled)
        corr_ref[row, :, at] = surface[:4].astype(BF16)
        corr_ref[row + 1, :, at] = surface[4:].astype(BF16)

    group = 16

    def group_step(number, carry):
        for k in range(0, group, 2):
            for piece in range(cols // step):
                pair(number * group + k, piece)
        return carry

    lax.fori_loop(0, rows // group, group_step, 0)


def correct_near_kernel(*refs):
    correct_rows(0, *refs)


def segment_list(near_ref, far_ref):
    each = far_ref.shape[0] // SEG
    shift = jnp.where(is_half(0), each, 0)
    return [(shift + k, near_ref, k) for k in range(each)] + [(each - shift + k, far_ref, k) for k in range(each)]


def correct_far_kernel(routes_in_ref, starts_in_ref, *refs):
    near_ref, corr_ref, sides = refs[8], refs[9], refs[10:14]
    pos_ref, routes_ref, starts_ref, sems = refs[14:]
    copies = [
        pltpu.make_async_copy(routes_in_ref, routes_ref, sems.at[0]),
        pltpu.make_async_copy(starts_in_ref, starts_ref, sems.at[1]),
    ]
    for copy in copies:
        copy.start()
    correct_rows(1, *refs[:8], corr_ref, pos_ref)
    for copy in copies:
        copy.wait()
    me = lax.axis_index("along")
    beside = 1 - 2 * (me % 2)
    beyond = 2 - 4 * ((me // 2) % 2)
    listed = segment_list(near_ref, corr_ref)
    band = lax.broadcasted_iota(jnp.int32, corr_ref.shape[1:], 0)
    for target, out_ref in zip((me + beside, me - beside, me + beyond, me - beyond), sides):
        count = jnp.int32(0)
        tags = [jnp.int32(0) for _ in range(CAP)]
        for segment, from_ref, place in listed:
            hit = routes_ref[1, segment] == target
            slot = count

            @pl.when(hit)
            def _():
                out_ref[pl.ds(slot * SEG, SEG)] = from_ref[place * SEG : (place + 1) * SEG]

            tag = jnp.where(hit, starts_ref[1, segment] + 1, 0)
            tags = [jnp.where(slot == k, tags[k] + tag, tags[k]) for k in range(CAP)]
            count = count + hit.astype(jnp.int32)
        line = jnp.zeros(band.shape, jnp.int32)
        for k in range(CAP):
            line = jnp.where(band == k, tags[k], line)
        out_ref[CAP * SEG] = line.astype(F32).astype(BF16)


def add_rows(acc_ref, start, from_ref, place):
    for row in range(SEG):
        acc_ref[start + row] = acc_ref[start + row] + from_ref[place * SEG + row].astype(F32)


def covers(rows, start):
    line = lax.broadcasted_iota(jnp.int32, (rows, LANES), 0)
    return jnp.where((line >= start) & (line < start + SEG), 1.0, 0.0)


def read_tags(side_refs):
    found = []
    for side_ref in side_refs:
        tags = side_ref[CAP * SEG, :, :LANES].astype(F32)
        band = lax.broadcasted_iota(jnp.int32, tags.shape, 0)
        for slot in range(CAP):
            found.append((jnp.max(jnp.where(band == slot, tags, 0.0)).astype(jnp.int32), side_ref, slot))
    return found


def add_sides(acc_ref, count, side_refs):
    found = read_tags(side_refs)
    for tag, side_ref, slot in found:
        start = jnp.maximum(tag - 1, 0)
        count = count + jnp.where(tag > 0, covers(count.shape[0], start), 0.0)

        @pl.when(tag > 0)
        def _():
            add_rows(acc_ref, start, side_ref, slot)

    return count


def own_kernel(starts_ref, near_ref, far_ref, acc_ref, count_ref):
    acc_ref[...] = jnp.zeros(acc_ref.shape, F32)
    count = jnp.zeros(count_ref.shape, F32)
    listed = segment_list(near_ref, far_ref)
    for segment, from_ref, place in listed:
        start = starts_ref[0, segment]
        count = count + covers(count.shape[0], start)
        add_rows(acc_ref, start, from_ref, place)
    count_ref[...] = count


def add_kernel(acc_in_ref, count_in_ref, side0_ref, side1_ref, acc_ref, count_ref):
    count_ref[...] = add_sides(acc_ref, count_in_ref[...], (side0_ref, side1_ref))


def last_kernel(acc_in_ref, count_in_ref, side0_ref, side1_ref, acc_ref, out_ref, inv_ref, line_ref, sems):
    count = add_sides(acc_ref, count_in_ref[...], (side0_ref, side1_ref))
    inv_ref[...] = 1.0 / jnp.maximum(count, 1.0)
    rows, bands, cols = line_ref.shape
    size = rows // 4
    copies = []
    for part in range(4):
        for row in range(part * size, (part + 1) * size):
            inverse = jnp.broadcast_to(inv_ref[row : row + 1, :], (bands, LANES))
            inverse = jnp.concatenate([inverse] * (cols // LANES), axis=1)
            line_ref[row] = (acc_ref[row] * inverse).astype(BF16)
        at = pl.ds(part * size, size)
        copies.append(pltpu.make_async_copy(line_ref.at[at], out_ref.at[at], sems.at[part]))
        copies[-1].start()
    for copy in copies:
        copy.wait()


def body(
    toa_bands,
    dark_mask,
    vapour,
    elev_class,
    elev_frac,
    kernel,
    lut_gain,
    lut_path,
    lut_albedo,
    routes,
    starts,
):
    rows, bands, cols = toa_bands.shape
    levels_e, levels_a, levels_w = lut_gain.shape[1:]
    nodes = levels_a * levels_w
    count = lax.axis_size("along")
    half = rows // 2
    fields = jax.ShapeDtypeStruct((2, half, cols), BF16)
    near_out, far_out = pl.pallas_call(
        prep_kernel,
        out_shape=(fields, fields),
        in_specs=[HBM, HBM],
        out_specs=(VMEM, VMEM),
        scratch_shapes=[
            pltpu.VMEM((rows, bands, cols), BF16),
            pltpu.VMEM((rows, cols), jnp.int32),
            pltpu.SemaphoreType.DMA((2, 4)),
        ],
        compiler_params=params(),
        name="prep",
    )(*in_hbm(toa_bands, dark_mask))
    near_in = lax.ppermute(near_out, "along", swap_pairs(count, 1, 0))
    far_in = lax.ppermute(far_out, "along", swap_pairs(count, 1, 1))
    block = 256
    weights = (
        jax.ShapeDtypeStruct((levels_w, half, cols), F32),
        jax.ShapeDtypeStruct((half, cols), F32),
    )
    tables = [table.transpose(0, 1, 3, 2).reshape(-1, levels_a) for table in (lut_gain, lut_path, lut_albedo)]
    whole = jax.ShapeDtypeStruct((rows, cols), F32)
    lut, row_bands, col_bands, vapours, classes, fracs = pl.pallas_call(
        functools.partial(early_kernel, (bands, levels_e, levels_w, levels_a)),
        out_shape=(
            jax.ShapeDtypeStruct((6 * levels_e * bands, 2 * nodes), BF16),
            jax.ShapeDtypeStruct((2, half, 3 * half), BF16),
            jax.ShapeDtypeStruct((2, block, block + 2 * LANES), BF16),
            whole,
            jax.ShapeDtypeStruct((rows, cols), jnp.int32),
            whole,
        ),
        in_specs=[HBM] * 7,
        out_specs=(VMEM,) * 6,
        scratch_shapes=[
            pltpu.VMEM((3, bands * levels_e * levels_w, levels_a), BF16),
            pltpu.VMEM((1, kernel.shape[0]), F32),
            pltpu.SemaphoreType.DMA((7,)),
        ],
        compiler_params=params(),
        name="early",
    )(*in_hbm(*tables, kernel[None, :], vapour, elev_class, elev_frac))

    def smooth_rows(flip, here, beside, incoming, *after):
        ext, edge = pl.pallas_call(
            functools.partial(vertical_kernel, flip),
            out_shape=(
                jax.ShapeDtypeStruct((2, 2, half, cols), BF16),
                jax.ShapeDtypeStruct((2, half, LANES), F32),
            ),
            in_specs=[VMEM] * (4 + len(after)),
            out_specs=(VMEM, VMEM),
            compiler_params=params(),
            name="vertical",
        )(row_bands, here, beside, incoming, *after)
        hats = pl.pallas_call(
            functools.partial(hats_kernel, flip),
            out_shape=weights,
            in_specs=[VMEM] * 4,
            out_specs=(VMEM, VMEM),
            compiler_params=params(),
            name="hats",
        )(vapours, classes, fracs, edge)
        return lax.ppermute(edge, "across", swap_pairs(lax.axis_size("across"), 1, 0)), ext, *hats


    corrected = jax.ShapeDtypeStruct((half, bands, cols), BF16)
    scratch = [pltpu.VMEM((half, cols), F32)]
    near_corr = pl.pallas_call(
        correct_near_kernel,
        out_shape=corrected,
        in_specs=[VMEM] * 8,
        out_specs=VMEM,
        scratch_shapes=scratch,
        compiler_params=params(),
        name="correct_near",
    )(col_bands, lut, *smooth_rows(0, near_out, far_out, near_in), toa_bands, classes)
    far = smooth_rows(1, far_out, near_out, far_in, near_corr)
    segments = rows // SEG
    slots = jax.ShapeDtypeStruct((CAP * SEG + 1, bands, cols), BF16)
    far_corr, *sides = pl.pallas_call(
        correct_far_kernel,
        out_shape=(corrected,) + (slots,) * 4,
        in_specs=[HBM, HBM] + [VMEM] * 9,
        out_specs=(VMEM,) * 5,
        scratch_shapes=scratch
        + [pltpu.SMEM((2, segments), jnp.int32)] * 2
        + [pltpu.SemaphoreType.DMA((2,))],
        compiler_params=params(),
        name="correct_far",
    )(*in_hbm(routes.T, starts.T), col_bands, lut, *far, toa_bands, classes, near_corr)
    moves = ((1, 0), (1, 1), (2, 0), (2, 1))
    got = [
        lax.ppermute(side, "along", swap_pairs(count, step, offset)) for side, (step, offset) in zip(sides, moves)
    ]
    total = jax.ShapeDtypeStruct((rows, bands, cols), F32)
    counts = jax.ShapeDtypeStruct((rows, LANES), F32)
    acc, number = pl.pallas_call(
        own_kernel,
        out_shape=(total, counts),
        in_specs=[SMEM, VMEM, VMEM],
        out_specs=(VMEM, VMEM),
        compiler_params=params(),
        name="own",
    )(starts.T, near_corr, far_corr)
    acc, number = pl.pallas_call(
        add_kernel,
        out_shape=(total, counts),
        in_specs=[VMEM] * 4,
        out_specs=(VMEM, VMEM),
        input_output_aliases={0: 0, 1: 1},
        compiler_params=params(),
        name="add",
    )(acc, number, got[0], got[1])
    _, out = pl.pallas_call(
        last_kernel,
        out_shape=(total, jax.ShapeDtypeStruct((rows, bands, cols), BF16)),
        in_specs=[VMEM] * 4,
        out_specs=(VMEM, HBM),
        scratch_shapes=[
            pltpu.VMEM((rows, LANES), F32),
            pltpu.VMEM((rows, bands, cols), BF16),
            pltpu.SemaphoreType.DMA((4,)),
        ],
        input_output_aliases={0: 0},
        compiler_params=params(),
        name="last",
    )(acc, number, got[2], got[3])
    return out[None]


def solution(mesh):
    in_specs = (
        P(("groups", "along"), None, "across"),
        P(("groups", "along"), "across"),
        P(("groups", "along"), "across"),
        P(("groups", "along"), "across"),
        P(("groups", "along"), "across"),
        P(),
        P(),
        P(),
        P(),
        P(("groups", "along"), None),
        P(("groups", "along"), None),
    )
    out_specs = P(("groups", "along"), None, None, "across")
    return jax.shard_map(body, mesh=mesh, in_specs=in_specs, out_specs=out_specs, check_vma=False)
```

```python
import functools

import jax
import jax.numpy as jnp
from jax import lax
from jax.experimental import pallas as pl
from jax.experimental.pallas import tpu as pltpu
from jax.sharding import PartitionSpec as P

SEG = 16
CAP = 2
LANES = 128

F32 = jnp.float32
BF16 = jnp.bfloat16
VMEM = pl.BlockSpec(memory_space=pltpu.VMEM)
HBM = pl.BlockSpec(memory_space=pltpu.HBM)
SMEM = pl.BlockSpec(memory_space=pltpu.SMEM)


def params(mib=24):
    return pltpu.CompilerParams(vmem_limit_bytes=mib * 1024 * 1024)


def swap_pairs(count, step, offset):
    pairs = []
    for i in range(count - step):
        if (i // step) % 2 == offset:
            pairs += [(i, i + step), (i + step, i)]
    return pairs


def in_hbm(*arrays):
    return [pltpu.with_memory_space_constraint(array, pltpu.HBM) for array in arrays]


def split_bf16(x):
    high = x.astype(BF16)
    return high, (x - high.astype(F32)).astype(BF16)


def prep_kernel(toa_ref, dark_ref, near_ref, far_ref, toa_in, dark_in, sems):
    rows = toa_in.shape[0]
    parts = 4
    size = rows // parts
    even = lax.axis_index("along") % 2 == 0
    copies = []
    for part in range(parts):
        at = pl.ds(part * size, size)
        copies.append(
            (
                pltpu.make_async_copy(toa_ref.at[at], toa_in.at[at], sems.at[0, part]),
                pltpu.make_async_copy(dark_ref.at[at], dark_in.at[at], sems.at[1, part]),
            )
        )
        for copy in copies[-1]:
            copy.start()
    for part in range(parts):
        for copy in copies[part]:
            copy.wait()
        at = slice(part * size, (part + 1) * size)
        to = slice(part % 2 * size, (part % 2 + 1) * size)
        into_near = even if part >= 2 else jnp.logical_not(even)
        dark = dark_in[at].astype(F32)
        lines = [(toa_in[at, band, :].astype(F32) * dark).astype(BF16) for band in (0, 2)]
        for flag, out_ref in ((into_near, near_ref), (jnp.logical_not(into_near), far_ref)):

            @pl.when(flag)
            def _():
                for field in range(2):
                    out_ref[field, to] = lines[field]


def store_bands(taps, out_ref, first):
    depth, width = out_ref.shape[1], out_ref.shape[2]
    taps = jnp.concatenate([taps, jnp.zeros((1, LANES - taps.shape[1]), F32)], axis=1)
    base = taps
    if width > LANES:
        base = jnp.concatenate([taps, jnp.zeros((1, width - LANES), F32)], axis=1)
    base = jnp.broadcast_to(base, (8, base.shape[1]))
    base = pltpu.roll(base, 0, 1, stride=1, stride_axis=0)
    for at in range(0, depth, 16):
        pair = [pltpu.roll(base, first + at + 8 * k, 1)[:, :width] for k in range(2)]
        high, low = split_bf16(jnp.concatenate(pair, axis=0))
        out_ref[0, at : at + 16] = high
        out_ref[1, at : at + 16] = low


def is_half(flip):
    return lax.axis_index("along") % 2 == flip


def vertical_kernel(flip, bands_ref, here_ref, beside_ref, in_ref, *rest):
    ext_ref, edge_ref = rest[-2:]
    lower = is_half(flip)
    left = lax.axis_index("across") == 0
    size = bands_ref.shape[1]
    matrix = jnp.concatenate([bands_ref[0], bands_ref[1]], axis=0)

    def field(index):
        beside, incoming = beside_ref[index], in_ref[index]
        return jnp.concatenate(
            [jnp.where(lower, beside, incoming), here_ref[index], jnp.where(lower, incoming, beside)], axis=0
        )

    def smooth(block):
        both = jnp.dot(matrix, block, preferred_element_type=F32)
        return both[:size] + both[size:]

    blue, red = field(0), field(1)
    dark = jnp.where(blue.astype(F32) > 0.0, 1.0, 0.0).astype(BF16)
    for index, value in enumerate((8.0 * (smooth(blue) - 0.5 * smooth(red)), smooth(dark))):
        edge_ref[index] = jnp.where(left, value[:, -LANES:], value[:, :LANES])
        high, low = split_bf16(value)
        ext_ref[0, index] = high
        ext_ref[1, index] = low


def store_table(array, out_ref, table, shape):
    bands, levels_e, levels_w, levels_a = shape
    nodes = levels_w * levels_a

    def iota(size, dim):
        return lax.broadcasted_iota(jnp.int32, size, dim)

    repeat = iota((levels_a, nodes), 1) % levels_a == iota((levels_a, nodes), 0)
    spread = jnp.dot(array, jnp.where(repeat, 1.0, 0.0).astype(BF16), preferred_element_type=F32)
    own = iota(spread.shape, 1) // levels_a == iota(spread.shape, 0) % levels_w
    spread = jnp.where(own, spread, 0.0).astype(BF16)
    size = (2 * bands * levels_e, spread.shape[0])
    row, source = iota(size, 0), iota(size, 1) // levels_w
    wanted = row % bands * levels_e + row // (2 * bands)
    for k in range(2):
        pick = (source == wanted) & (row // bands % 2 == k)
        part = jnp.dot(jnp.where(pick, 1.0, 0.0).astype(BF16), spread, preferred_element_type=F32)
        out_ref[table * size[0] : (table + 1) * size[0], k * nodes : (k + 1) * nodes] = part.astype(BF16)


def early_kernel(taps_ref, *refs):
    count = (len(refs) - 3) // 2
    sources, results, (rows_ref, taps_out_ref, sems) = refs[:count], refs[count : 2 * count], refs[2 * count :]
    pairs = [(taps_ref, taps_out_ref)] + list(zip(sources, results))
    copies = [pltpu.make_async_copy(source, into, sems.at[k]) for k, (source, into) in enumerate(pairs)]
    for copy in copies:
        copy.start()
    copies[0].wait()
    store_bands(taps_out_ref[...], rows_ref, rows_ref.shape[1] - 30)
    for copy in copies[1:]:
        copy.wait()


def tables_kernel(shape, taps_ref, gain_ref, path_ref, albedo_ref, *rest):
    lut_ref, cols_ref = rest[-2:]
    store_bands(taps_ref[...], cols_ref, LANES - 30)
    for number, table_ref in enumerate((gain_ref, path_ref, albedo_ref)):
        store_table(table_ref[...], lut_ref, number, shape)


def hats_kernel(flip, vapour_ref, class_ref, frac_ref, *rest):
    hat_ref, even_ref = rest[-2:]
    rows = even_ref.shape[0]
    here = pl.ds(pl.multiple_of(jnp.where(is_half(flip), rows, 0), rows), rows)
    vapour = vapour_ref[here]
    for w in range(hat_ref.shape[0]):
        hat_ref[w] = jnp.maximum(0.0, 1.0 - jnp.abs(vapour - float(w)))
    frac = frac_ref[here]
    even_ref[...] = jnp.where(class_ref[here] % 2 == 0, 1.0 - frac, frac)


def correct_rows(
    flip,
    bands_ref,
    lut_ref,
    edge_ref,
    ext_ref,
    hat_ref,
    even_ref,
    toa_ref,
    class_ref,
    corr_ref,
    pos_ref,
):
    rows, cols = pos_ref.shape
    base = pl.multiple_of(jnp.where(is_half(flip), rows, 0), rows)
    left = lax.axis_index("across") == 0
    levels_w = hat_ref.shape[0]
    levels_a = lut_ref.shape[1] // (2 * levels_w)
    block = bands_ref.shape[1]
    window = bands_ref.shape[2]
    lines = []
    for index in range(2):
        terms = split_bf16(edge_ref[index])
        for k in range(2):
            none = jnp.zeros_like(terms[k])
            lines.append((jnp.where(left, none, terms[k]), ext_ref[k, index], jnp.where(left, terms[k], none)))
    lines = [jnp.concatenate(line, axis=1) for line in (lines[0], lines[2], lines[1], lines[3])]
    windows = [slice(number * block, number * block + window) for number in range(cols // block)]
    contract = (((1,), (1,)), ((), ()))
    every = jnp.concatenate([line[:, at] for line in lines for at in windows], axis=0)
    full = lax.dot_general(every, bands_ref[0], contract, preferred_element_type=F32)
    rest = lax.dot_general(every[: every.shape[0] // 2], bands_ref[1], contract, preferred_element_type=F32)
    pieces = len(windows)
    for number in range(pieces):
        at = slice(number * block, (number + 1) * block)

        def part(array, line):
            return array[(line * pieces + number) * rows : (line * pieces + number + 1) * rows]

        weighted = part(full, 0) + (part(full, 2) + part(rest, 0))
        darkness = part(full, 1) + (part(full, 3) + part(rest, 1))
        aerosol = weighted / jnp.maximum(darkness, 1.0)
        pos_ref[:, at] = (levels_a - 1.0) / (1.0 + jnp.exp(-aerosol))

    step = 256
    node_a = lax.broadcasted_iota(jnp.int32, (levels_a, step), 0).astype(F32)
    second = lax.broadcasted_iota(jnp.int32, (8, step), 0) >= 4
    lut = lut_ref[...]

    def pair(row, number):
        at = slice(number * step, (number + 1) * step)
        pieces = []
        for k in range(2):
            one = pl.ds(row + k, 1)
            hat_a = jnp.maximum(0.0, 1.0 - jnp.abs(pos_ref[one, at] - node_a)).astype(BF16)
            pieces += [
                hat_a * jnp.broadcast_to(hat_ref[w, one, at], (levels_a, step)).astype(BF16) for w in range(levels_w)
            ]
        nodes = jnp.dot(lut, jnp.concatenate(pieces, axis=0), preferred_element_type=F32)

        def both(ref, first):
            one, two = (jnp.broadcast_to(ref[pl.ds(first + k, 1), at], (8, step)) for k in range(2))
            return jnp.where(second, two, one)

        level = both(class_ref, base + row)
        w_even = both(even_ref, row)
        w_odd = 1.0 - w_even
        below = [level < k for k in range(7)]

        def coefficient(table):
            node = [nodes[64 * table + 8 * k : 64 * table + 8 * k + 8] for k in range(8)]
            even = jnp.where(
                below[3], jnp.where(below[1], node[0], node[2]), jnp.where(below[5], node[4], node[6])
            )
            odd = jnp.where(
                below[4], jnp.where(below[2], node[1], node[3]), jnp.where(below[6], node[5], node[7])
            )
            return w_even * even + w_odd * odd

        toa = jnp.concatenate([toa_ref[base + row + k, :, at].astype(F32) for k in range(2)], axis=0)
        scaled = coefficient(0) * toa - coefficient(1)
        surface = scaled / (1.0 + coefficient(2) * scaled)
        corr_ref[row, :, at] = surface[:4].astype(BF16)
        corr_ref[row + 1, :, at] = surface[4:].astype(BF16)

    group = 16

    def group_step(number, carry):
        for k in range(0, group, 2):
            for piece in range(cols // step):
                pair(number * group + k, piece)
        return carry

    lax.fori_loop(0, rows // group, group_step, 0)


def correct_near_kernel(*refs):
    correct_rows(0, *refs)


def segment_list(near_ref, far_ref):
    each = far_ref.shape[0] // SEG
    shift = jnp.where(is_half(0), each, 0)
    return [(shift + k, near_ref, k) for k in range(each)] + [(each - shift + k, far_ref, k) for k in range(each)]


def correct_far_kernel(routes_in_ref, starts_in_ref, *refs):
    near_ref, corr_ref, sides = refs[8], refs[9], refs[10:14]
    pos_ref, routes_ref, starts_ref, sems = refs[14:]
    copies = [
        pltpu.make_async_copy(routes_in_ref, routes_ref, sems.at[0]),
        pltpu.make_async_copy(starts_in_ref, starts_ref, sems.at[1]),
    ]
    for copy in copies:
        copy.start()
    correct_rows(1, *refs[:8], corr_ref, pos_ref)
    for copy in copies:
        copy.wait()
    me = lax.axis_index("along")
    beside = 1 - 2 * (me % 2)
    beyond = 2 - 4 * ((me // 2) % 2)
    listed = segment_list(near_ref, corr_ref)
    band = lax.broadcasted_iota(jnp.int32, corr_ref.shape[1:], 0)
    for target, out_ref in zip((me + beside, me - beside, me + beyond, me - beyond), sides):
        count = jnp.int32(0)
        tags = [jnp.int32(0) for _ in range(CAP)]
        for segment, from_ref, place in listed:
            hit = routes_ref[1, segment] == target
            slot = count

            @pl.when(hit)
            def _():
                out_ref[pl.ds(slot * SEG, SEG)] = from_ref[place * SEG : (place + 1) * SEG]

            tag = jnp.where(hit, starts_ref[1, segment] + 1, 0)
            tags = [jnp.where(slot == k, tags[k] + tag, tags[k]) for k in range(CAP)]
            count = count + hit.astype(jnp.int32)
        line = jnp.zeros(band.shape, jnp.int32)
        for k in range(CAP):
            line = jnp.where(band == k, tags[k], line)
        out_ref[CAP * SEG] = line.astype(F32).astype(BF16)


def add_rows(acc_ref, start, from_ref, place):
    for row in range(SEG):
        acc_ref[start + row] = acc_ref[start + row] + from_ref[place * SEG + row].astype(F32)


def covers(rows, start):
    line = lax.broadcasted_iota(jnp.int32, (rows, LANES), 0)
    return jnp.where((line >= start) & (line < start + SEG), 1.0, 0.0)


def read_tags(side_refs):
    found = []
    for side_ref in side_refs:
        tags = side_ref[CAP * SEG, :, :LANES].astype(F32)
        band = lax.broadcasted_iota(jnp.int32, tags.shape, 0)
        for slot in range(CAP):
            found.append((jnp.max(jnp.where(band == slot, tags, 0.0)).astype(jnp.int32), side_ref, slot))
    return found


def add_sides(acc_ref, count, side_refs):
    found = read_tags(side_refs)
    for tag, side_ref, slot in found:
        start = jnp.maximum(tag - 1, 0)
        count = count + jnp.where(tag > 0, covers(count.shape[0], start), 0.0)

        @pl.when(tag > 0)
        def _():
            add_rows(acc_ref, start, side_ref, slot)

    return count


def own_kernel(starts_ref, near_ref, far_ref, acc_ref, count_ref):
    acc_ref[...] = jnp.zeros(acc_ref.shape, F32)
    count = jnp.zeros(count_ref.shape, F32)
    listed = segment_list(near_ref, far_ref)
    for segment, from_ref, place in listed:
        start = starts_ref[0, segment]
        count = count + covers(count.shape[0], start)
        add_rows(acc_ref, start, from_ref, place)
    count_ref[...] = count


def add_kernel(acc_in_ref, count_in_ref, side0_ref, side1_ref, acc_ref, count_ref):
    count_ref[...] = add_sides(acc_ref, count_in_ref[...], (side0_ref, side1_ref))


def last_kernel(acc_in_ref, count_in_ref, side0_ref, side1_ref, acc_ref, out_ref, inv_ref, line_ref, sems):
    count = add_sides(acc_ref, count_in_ref[...], (side0_ref, side1_ref))
    inv_ref[...] = 1.0 / jnp.maximum(count, 1.0)
    rows, bands, cols = line_ref.shape
    size = rows // 4
    copies = []
    for part in range(4):
        for row in range(part * size, (part + 1) * size):
            inverse = jnp.broadcast_to(inv_ref[row : row + 1, :], (bands, LANES))
            inverse = jnp.concatenate([inverse] * (cols // LANES), axis=1)
            line_ref[row] = (acc_ref[row] * inverse).astype(BF16)
        at = pl.ds(part * size, size)
        copies.append(pltpu.make_async_copy(line_ref.at[at], out_ref.at[at], sems.at[part]))
        copies[-1].start()
    for copy in copies:
        copy.wait()


def body(
    toa_bands,
    dark_mask,
    vapour,
    elev_class,
    elev_frac,
    kernel,
    lut_gain,
    lut_path,
    lut_albedo,
    routes,
    starts,
):
    rows, bands, cols = toa_bands.shape
    levels_e, levels_a, levels_w = lut_gain.shape[1:]
    nodes = levels_a * levels_w
    count = lax.axis_size("along")
    half = rows // 2
    fields = jax.ShapeDtypeStruct((2, half, cols), BF16)
    near_out, far_out = pl.pallas_call(
        prep_kernel,
        out_shape=(fields, fields),
        in_specs=[HBM, HBM],
        out_specs=(VMEM, VMEM),
        scratch_shapes=[
            pltpu.VMEM((rows, bands, cols), BF16),
            pltpu.VMEM((rows, cols), jnp.int32),
            pltpu.SemaphoreType.DMA((2, 4)),
        ],
        compiler_params=params(),
        name="prep",
    )(*in_hbm(toa_bands, dark_mask))
    near_in = lax.ppermute(near_out, "along", swap_pairs(count, 1, 0))
    far_in = lax.ppermute(far_out, "along", swap_pairs(count, 1, 1))
    block = 256
    weights = (
        jax.ShapeDtypeStruct((levels_w, half, cols), F32),
        jax.ShapeDtypeStruct((half, cols), F32),
    )
    tables = [table.transpose(0, 1, 3, 2).reshape(-1, levels_a) for table in (lut_gain, lut_path, lut_albedo)]
    whole = jax.ShapeDtypeStruct((rows, cols), F32)
    whole_int = jax.ShapeDtypeStruct((rows, cols), jnp.int32)
    brought = [jax.ShapeDtypeStruct(table.shape, BF16) for table in tables] + [whole, whole_int, whole]
    *tables, vapours, classes, fracs, row_bands, taps = pl.pallas_call(
        early_kernel,
        out_shape=(
            *brought,
            jax.ShapeDtypeStruct((2, half, 3 * half), BF16),
            jax.ShapeDtypeStruct((1, kernel.shape[0]), F32),
        ),
        in_specs=[HBM] * 7,
        out_specs=(VMEM,) * 8,
        scratch_shapes=[pltpu.SemaphoreType.DMA((7,))],
        compiler_params=params(),
        name="early",
    )(*in_hbm(kernel[None, :], *tables, vapour, elev_class, elev_frac))

    def smooth_rows(flip, here, beside, incoming, *after):
        ext, edge = pl.pallas_call(
            functools.partial(vertical_kernel, flip),
            out_shape=(
                jax.ShapeDtypeStruct((2, 2, half, cols), BF16),
                jax.ShapeDtypeStruct((2, half, LANES), F32),
            ),
            in_specs=[VMEM] * (4 + len(after)),
            out_specs=(VMEM, VMEM),
            compiler_params=params(),
            name="vertical",
        )(row_bands, here, beside, incoming, *after)
        hats = pl.pallas_call(
            functools.partial(hats_kernel, flip),
            out_shape=weights,
            in_specs=[VMEM] * 4,
            out_specs=(VMEM, VMEM),
            compiler_params=params(),
            name="hats",
        )(vapours, classes, fracs, edge)
        return edge, lax.ppermute(edge, "across", swap_pairs(lax.axis_size("across"), 1, 0)), ext, *hats


    corrected = jax.ShapeDtypeStruct((half, bands, cols), BF16)
    scratch = [pltpu.VMEM((half, cols), F32)]
    sent, *near = smooth_rows(0, near_out, far_out, near_in)
    lut, col_bands = pl.pallas_call(
        functools.partial(tables_kernel, (bands, levels_e, levels_w, levels_a)),
        out_shape=(
            jax.ShapeDtypeStruct((6 * levels_e * bands, 2 * nodes), BF16),
            jax.ShapeDtypeStruct((2, block, block + 2 * LANES), BF16),
        ),
        in_specs=[VMEM] * 5,
        out_specs=(VMEM, VMEM),
        compiler_params=params(),
        name="tables",
    )(taps, *tables, sent)
    near_corr = pl.pallas_call(
        correct_near_kernel,
        out_shape=corrected,
        in_specs=[VMEM] * 8,
        out_specs=VMEM,
        scratch_shapes=scratch,
        compiler_params=params(),
        name="correct_near",
    )(col_bands, lut, *near, toa_bands, classes)
    _, *far = smooth_rows(1, far_out, near_out, far_in, near_corr)
    segments = rows // SEG
    slots = jax.ShapeDtypeStruct((CAP * SEG + 1, bands, cols), BF16)
    far_corr, *sides = pl.pallas_call(
        correct_far_kernel,
        out_shape=(corrected,) + (slots,) * 4,
        in_specs=[HBM, HBM] + [VMEM] * 9,
        out_specs=(VMEM,) * 5,
        scratch_shapes=scratch
        + [pltpu.SMEM((2, segments), jnp.int32)] * 2
        + [pltpu.SemaphoreType.DMA((2,))],
        compiler_params=params(),
        name="correct_far",
    )(*in_hbm(routes.T, starts.T), col_bands, lut, *far, toa_bands, classes, near_corr)
    moves = ((1, 0), (1, 1), (2, 0), (2, 1))
    got = [None] * 4
    for k in [0, 2, 1, 3]:
        step, offset = moves[k]
        got[k] = lax.ppermute(sides[k], "along", swap_pairs(count, step, offset))
    total = jax.ShapeDtypeStruct((rows, bands, cols), F32)
    counts = jax.ShapeDtypeStruct((rows, LANES), F32)
    acc, number = pl.pallas_call(
        own_kernel,
        out_shape=(total, counts),
        in_specs=[SMEM, VMEM, VMEM],
        out_specs=(VMEM, VMEM),
        compiler_params=params(),
        name="own",
    )(starts.T, near_corr, far_corr)
    acc, number = pl.pallas_call(
        add_kernel,
        out_shape=(total, counts),
        in_specs=[VMEM] * 4,
        out_specs=(VMEM, VMEM),
        input_output_aliases={0: 0, 1: 1},
        compiler_params=params(),
        name="add",
    )(acc, number, got[0], got[2])
    _, out = pl.pallas_call(
        last_kernel,
        out_shape=(total, jax.ShapeDtypeStruct((rows, bands, cols), BF16)),
        in_specs=[VMEM] * 4,
        out_specs=(VMEM, HBM),
        scratch_shapes=[
            pltpu.VMEM((rows, LANES), F32),
            pltpu.VMEM((rows, bands, cols), BF16),
            pltpu.SemaphoreType.DMA((4,)),
        ],
        input_output_aliases={0: 0},
        compiler_params=params(),
        name="last",
    )(acc, number, got[1], got[3])
    return out[None]


def solution(mesh):
    in_specs = (
        P(("groups", "along"), None, "across"),
        P(("groups", "along"), "across"),
        P(("groups", "along"), "across"),
        P(("groups", "along"), "across"),
        P(("groups", "along"), "across"),
        P(),
        P(),
        P(),
        P(),
        P(("groups", "along"), None),
        P(("groups", "along"), None),
    )
    out_specs = P(("groups", "along"), None, None, "across")
    return jax.shard_map(body, mesh=mesh, in_specs=in_specs, out_specs=out_specs, check_vma=False)
```

```python
import functools

import jax
import jax.numpy as jnp
from jax import lax
from jax.experimental import pallas as pl
from jax.experimental.pallas import tpu as pltpu
from jax.sharding import PartitionSpec as P

SEG = 16
CAP = 2
LANES = 128

F32 = jnp.float32
BF16 = jnp.bfloat16
VMEM = pl.BlockSpec(memory_space=pltpu.VMEM)
HBM = pl.BlockSpec(memory_space=pltpu.HBM)
SMEM = pl.BlockSpec(memory_space=pltpu.SMEM)


def params(mib=24):
    return pltpu.CompilerParams(vmem_limit_bytes=mib * 1024 * 1024)


def swap_pairs(count, step, offset):
    pairs = []
    for i in range(count - step):
        if (i // step) % 2 == offset:
            pairs += [(i, i + step), (i + step, i)]
    return pairs


def in_hbm(*arrays):
    return [pltpu.with_memory_space_constraint(array, pltpu.HBM) for array in arrays]


def split_bf16(x):
    high = x.astype(BF16)
    return high, (x - high.astype(F32)).astype(BF16)


def prep_kernel(toa_ref, dark_ref, near_ref, far_ref, toa_in, dark_in, sems):
    rows = toa_in.shape[0]
    parts = 4
    size = rows // parts
    even = lax.axis_index("along") % 2 == 0
    copies = []
    for part in range(parts):
        at = pl.ds(part * size, size)
        copies.append(
            (
                pltpu.make_async_copy(toa_ref.at[at], toa_in.at[at], sems.at[0, part]),
                pltpu.make_async_copy(dark_ref.at[at], dark_in.at[at], sems.at[1, part]),
            )
        )
        for copy in copies[-1]:
            copy.start()
    for part in range(parts):
        for copy in copies[part]:
            copy.wait()
        at = slice(part * size, (part + 1) * size)
        to = slice(part % 2 * size, (part % 2 + 1) * size)
        into_near = even if part >= 2 else jnp.logical_not(even)
        dark = dark_in[at].astype(F32)
        lines = [(toa_in[at, band, :].astype(F32) * dark).astype(BF16) for band in (0, 2)]
        for flag, out_ref in ((into_near, near_ref), (jnp.logical_not(into_near), far_ref)):

            @pl.when(flag)
            def _():
                for field in range(2):
                    out_ref[field, to] = lines[field]


def store_bands(taps, out_ref, first):
    depth, width = out_ref.shape[1], out_ref.shape[2]
    taps = jnp.concatenate([taps, jnp.zeros((1, LANES - taps.shape[1]), F32)], axis=1)
    base = taps
    if width > LANES:
        base = jnp.concatenate([taps, jnp.zeros((1, width - LANES), F32)], axis=1)
    base = jnp.broadcast_to(base, (8, base.shape[1]))
    base = pltpu.roll(base, 0, 1, stride=1, stride_axis=0)
    for at in range(0, depth, 16):
        pair = [pltpu.roll(base, first + at + 8 * k, 1)[:, :width] for k in range(2)]
        high, low = split_bf16(jnp.concatenate(pair, axis=0))
        out_ref[0, at : at + 16] = high
        out_ref[1, at : at + 16] = low


def is_half(flip):
    return lax.axis_index("along") % 2 == flip


def vertical_kernel(flip, bands_ref, here_ref, beside_ref, in_ref, *rest):
    ext_ref, edge_ref = rest[-2:]
    lower = is_half(flip)
    left = lax.axis_index("across") == 0
    size = bands_ref.shape[1]
    matrix = jnp.concatenate([bands_ref[0], bands_ref[1]], axis=0)

    def field(index):
        beside, incoming = beside_ref[index], in_ref[index]
        return jnp.concatenate(
            [jnp.where(lower, beside, incoming), here_ref[index], jnp.where(lower, incoming, beside)], axis=0
        )

    def smooth(block):
        both = jnp.dot(matrix, block, preferred_element_type=F32)
        return both[:size] + both[size:]

    blue, red = field(0), field(1)
    dark = jnp.where(blue.astype(F32) > 0.0, 1.0, 0.0).astype(BF16)
    for index, value in enumerate((8.0 * (smooth(blue) - 0.5 * smooth(red)), smooth(dark))):
        edge_ref[index] = jnp.where(left, value[:, -LANES:], value[:, :LANES])
        high, low = split_bf16(value)
        ext_ref[0, index] = high
        ext_ref[1, index] = low


def store_table(array, out_ref, table, shape):
    bands, levels_e, levels_w, levels_a = shape
    nodes = levels_w * levels_a

    def iota(size, dim):
        return lax.broadcasted_iota(jnp.int32, size, dim)

    repeat = iota((levels_a, nodes), 1) % levels_a == iota((levels_a, nodes), 0)
    spread = jnp.dot(array, jnp.where(repeat, 1.0, 0.0).astype(BF16), preferred_element_type=F32)
    own = iota(spread.shape, 1) // levels_a == iota(spread.shape, 0) % levels_w
    spread = jnp.where(own, spread, 0.0).astype(BF16)
    size = (2 * bands * levels_e, spread.shape[0])
    row, source = iota(size, 0), iota(size, 1) // levels_w
    wanted = row % bands * levels_e + row // (2 * bands)
    for k in range(2):
        pick = (source == wanted) & (row // bands % 2 == k)
        part = jnp.dot(jnp.where(pick, 1.0, 0.0).astype(BF16), spread, preferred_element_type=F32)
        out_ref[table * size[0] : (table + 1) * size[0], k * nodes : (k + 1) * nodes] = part.astype(BF16)


def early_kernel(taps_ref, *refs):
    count = (len(refs) - 3) // 2
    sources, results, (rows_ref, taps_out_ref, sems) = refs[:count], refs[count : 2 * count], refs[2 * count :]
    pairs = [(taps_ref, taps_out_ref)] + list(zip(sources, results))
    copies = [pltpu.make_async_copy(source, into, sems.at[k]) for k, (source, into) in enumerate(pairs)]
    for copy in copies:
        copy.start()
    copies[0].wait()
    store_bands(taps_out_ref[...], rows_ref, rows_ref.shape[1] - 30)
    for copy in copies[1:]:
        copy.wait()


def tables_kernel(shape, taps_ref, gain_ref, path_ref, albedo_ref, *rest):
    lut_ref, cols_ref = rest[-2:]
    store_bands(taps_ref[...], cols_ref, LANES - 30)
    for number, table_ref in enumerate((gain_ref, path_ref, albedo_ref)):
        store_table(table_ref[...], lut_ref, number, shape)


def hats_kernel(flip, vapour_ref, class_ref, frac_ref, *rest):
    hat_ref, even_ref = rest[-2:]
    rows = even_ref.shape[0]
    here = pl.ds(pl.multiple_of(jnp.where(is_half(flip), rows, 0), rows), rows)
    vapour = vapour_ref[here]
    for w in range(hat_ref.shape[0]):
        hat_ref[w] = jnp.maximum(0.0, 1.0 - jnp.abs(vapour - float(w)))
    frac = frac_ref[here]
    even_ref[...] = jnp.where(class_ref[here] % 2 == 0, 1.0 - frac, frac)


def smooth_cols(bands_ref, edge_ref, ext_ref, pos_ref, levels_a):
    rows, cols = pos_ref.shape
    left = lax.axis_index("across") == 0
    block = bands_ref.shape[1]
    window = bands_ref.shape[2]
    lines = []
    for index in range(2):
        terms = split_bf16(edge_ref[index])
        for k in range(2):
            none = jnp.zeros_like(terms[k])
            lines.append((jnp.where(left, none, terms[k]), ext_ref[k, index], jnp.where(left, terms[k], none)))
    lines = [jnp.concatenate(line, axis=1) for line in (lines[0], lines[2], lines[1], lines[3])]
    windows = [slice(number * block, number * block + window) for number in range(cols // block)]
    contract = (((1,), (1,)), ((), ()))
    every = jnp.concatenate([line[:, at] for line in lines for at in windows], axis=0)
    full = lax.dot_general(every, bands_ref[0], contract, preferred_element_type=F32)
    rest = lax.dot_general(every[: every.shape[0] // 2], bands_ref[1], contract, preferred_element_type=F32)
    pieces = len(windows)
    for number in range(pieces):
        at = slice(number * block, (number + 1) * block)

        def part(array, line):
            return array[(line * pieces + number) * rows : (line * pieces + number + 1) * rows]

        weighted = part(full, 0) + (part(full, 2) + part(rest, 0))
        darkness = part(full, 1) + (part(full, 3) + part(rest, 1))
        aerosol = weighted / jnp.maximum(darkness, 1.0)
        pos_ref[:, at] = (levels_a - 1.0) / (1.0 + jnp.exp(-aerosol))


def correct_rows(flip, first, lut_ref, hat_ref, even_ref, pos_ref, toa_ref, class_ref, corr_ref):
    rows = corr_ref.shape[0]
    half, cols = pos_ref.shape
    base = pl.multiple_of(jnp.where(is_half(flip), half, 0) + first, rows)
    levels_w = hat_ref.shape[0]
    levels_a = lut_ref.shape[1] // (2 * levels_w)
    step = 256
    node_a = lax.broadcasted_iota(jnp.int32, (levels_a, step), 0).astype(F32)
    second = lax.broadcasted_iota(jnp.int32, (8, step), 0) >= 4
    lut = lut_ref[...]

    def pair(row, number):
        at = slice(number * step, (number + 1) * step)
        pieces = []
        for k in range(2):
            hat_a = jnp.maximum(0.0, 1.0 - jnp.abs(pos_ref[pl.ds(first + row + k, 1), at] - node_a)).astype(BF16)
            pieces += [
                hat_a * jnp.broadcast_to(hat_ref[w, pl.ds(first + row + k, 1), at], (levels_a, step)).astype(BF16) for w in range(levels_w)
            ]
        nodes = jnp.dot(lut, jnp.concatenate(pieces, axis=0), preferred_element_type=F32)

        def both(ref, begin):
            one, two = (jnp.broadcast_to(ref[pl.ds(begin + k, 1), at], (8, step)) for k in range(2))
            return jnp.where(second, two, one)

        level = both(class_ref, base + row)
        w_even = both(even_ref, first + row)
        w_odd = 1.0 - w_even
        below = [level < k for k in range(7)]

        def coefficient(table):
            node = [nodes[64 * table + 8 * k : 64 * table + 8 * k + 8] for k in range(8)]
            even = jnp.where(
                below[3], jnp.where(below[1], node[0], node[2]), jnp.where(below[5], node[4], node[6])
            )
            odd = jnp.where(
                below[4], jnp.where(below[2], node[1], node[3]), jnp.where(below[6], node[5], node[7])
            )
            return w_even * even + w_odd * odd

        toa = jnp.concatenate([toa_ref[base + row + k, :, at].astype(F32) for k in range(2)], axis=0)
        scaled = coefficient(0) * toa - coefficient(1)
        surface = scaled / (1.0 + coefficient(2) * scaled)
        corr_ref[row, :, at] = surface[:4].astype(BF16)
        corr_ref[row + 1, :, at] = surface[4:].astype(BF16)

    group = 16

    def group_step(number, carry):
        for k in range(0, group, 2):
            for piece in range(cols // step):
                pair(number * group + k, piece)
        return carry

    lax.fori_loop(0, rows // group, group_step, 0)


def near_kernel(levels_a, bands_ref, lut_ref, edge_ref, ext_ref, hat_ref, even_ref, toa_ref, class_ref, corr_ref, pos_ref):
    smooth_cols(bands_ref, edge_ref, ext_ref, pos_ref, levels_a)
    correct_rows(0, 0, lut_ref, hat_ref, even_ref, pos_ref, toa_ref, class_ref, corr_ref)


def next_kernel(first, lut_ref, hat_ref, even_ref, pos_ref, toa_ref, class_ref, *rest):
    correct_rows(0, first, lut_ref, hat_ref, even_ref, pos_ref, toa_ref, class_ref, rest[-1])


def segment_list(near_refs, far_ref):
    each = far_ref.shape[0] // SEG
    shift = jnp.where(is_half(0), each, 0)
    near = [(shift + k, near_refs[k], 0) for k in range(each)]
    return near + [(each - shift + k, far_ref, k) for k in range(each)]


def correct_far_kernel(levels_a, routes_in_ref, starts_in_ref, *refs):
    near_refs, corr_ref, sides = refs[8:-9], refs[-9], refs[-8:-4]
    pos_ref, routes_ref, starts_ref, sems = refs[-4:]
    copies = [
        pltpu.make_async_copy(routes_in_ref, routes_ref, sems.at[0]),
        pltpu.make_async_copy(starts_in_ref, starts_ref, sems.at[1]),
    ]
    for copy in copies:
        copy.start()
    bands_ref, lut_ref, edge_ref, ext_ref, hat_ref, even_ref, toa_ref, class_ref = refs[:8]
    smooth_cols(bands_ref, edge_ref, ext_ref, pos_ref, levels_a)
    correct_rows(1, 0, lut_ref, hat_ref, even_ref, pos_ref, toa_ref, class_ref, corr_ref)
    for copy in copies:
        copy.wait()
    me = lax.axis_index("along")
    beside = 1 - 2 * (me % 2)
    beyond = 2 - 4 * ((me // 2) % 2)
    listed = segment_list(near_refs, corr_ref)
    band = lax.broadcasted_iota(jnp.int32, corr_ref.shape[1:], 0)
    for target, out_ref in zip((me + beside, me - beside, me + beyond, me - beyond), sides):
        count = jnp.int32(0)
        tags = [jnp.int32(0) for _ in range(CAP)]
        for segment, from_ref, place in listed:
            hit = routes_ref[1, segment] == target
            slot = count

            @pl.when(hit)
            def _():
                out_ref[pl.ds(slot * SEG, SEG)] = from_ref[place * SEG : (place + 1) * SEG]

            tag = jnp.where(hit, starts_ref[1, segment] + 1, 0)
            tags = [jnp.where(slot == k, tags[k] + tag, tags[k]) for k in range(CAP)]
            count = count + hit.astype(jnp.int32)
        line = jnp.zeros(band.shape, jnp.int32)
        for k in range(CAP):
            line = jnp.where(band == k, tags[k], line)
        out_ref[CAP * SEG] = line.astype(F32).astype(BF16)


def add_rows(acc_ref, start, from_ref, place):
    for row in range(SEG):
        acc_ref[start + row] = acc_ref[start + row] + from_ref[place * SEG + row].astype(F32)


def covers(rows, start):
    line = lax.broadcasted_iota(jnp.int32, (rows, LANES), 0)
    return jnp.where((line >= start) & (line < start + SEG), 1.0, 0.0)


def read_tags(side_refs):
    found = []
    for side_ref in side_refs:
        tags = side_ref[CAP * SEG, :, :LANES].astype(F32)
        band = lax.broadcasted_iota(jnp.int32, tags.shape, 0)
        for slot in range(CAP):
            found.append((jnp.max(jnp.where(band == slot, tags, 0.0)).astype(jnp.int32), side_ref, slot))
    return found


def add_sides(acc_ref, count, side_refs):
    found = read_tags(side_refs)
    for tag, side_ref, slot in found:
        start = jnp.maximum(tag - 1, 0)
        count = count + jnp.where(tag > 0, covers(count.shape[0], start), 0.0)

        @pl.when(tag > 0)
        def _():
            add_rows(acc_ref, start, side_ref, slot)

    return count


def own_kernel(starts_ref, *refs):
    far_ref, acc_ref, count_ref = refs[-3:]
    acc_ref[...] = jnp.zeros(acc_ref.shape, F32)
    count = jnp.zeros(count_ref.shape, F32)
    listed = segment_list(refs[:-3], far_ref)
    for segment, from_ref, place in listed:
        start = starts_ref[0, segment]
        count = count + covers(count.shape[0], start)
        add_rows(acc_ref, start, from_ref, place)
    count_ref[...] = count


def add_kernel(acc_in_ref, count_in_ref, side0_ref, side1_ref, acc_ref, count_ref):
    count_ref[...] = add_sides(acc_ref, count_in_ref[...], (side0_ref, side1_ref))


def last_kernel(acc_in_ref, count_in_ref, side0_ref, side1_ref, acc_ref, out_ref, inv_ref, line_ref, sems):
    count = add_sides(acc_ref, count_in_ref[...], (side0_ref, side1_ref))
    inv_ref[...] = 1.0 / jnp.maximum(count, 1.0)
    rows, bands, cols = line_ref.shape
    size = rows // 4
    copies = []
    for part in range(4):
        for row in range(part * size, (part + 1) * size):
            inverse = jnp.broadcast_to(inv_ref[row : row + 1, :], (bands, LANES))
            inverse = jnp.concatenate([inverse] * (cols // LANES), axis=1)
            line_ref[row] = (acc_ref[row] * inverse).astype(BF16)
        at = pl.ds(part * size, size)
        copies.append(pltpu.make_async_copy(line_ref.at[at], out_ref.at[at], sems.at[part]))
        copies[-1].start()
    for copy in copies:
        copy.wait()


def body(
    toa_bands,
    dark_mask,
    vapour,
    elev_class,
    elev_frac,
    kernel,
    lut_gain,
    lut_path,
    lut_albedo,
    routes,
    starts,
):
    rows, bands, cols = toa_bands.shape
    levels_e, levels_a, levels_w = lut_gain.shape[1:]
    nodes = levels_a * levels_w
    count = lax.axis_size("along")
    half = rows // 2
    fields = jax.ShapeDtypeStruct((2, half, cols), BF16)
    near_out, far_out = pl.pallas_call(
        prep_kernel,
        out_shape=(fields, fields),
        in_specs=[HBM, HBM],
        out_specs=(VMEM, VMEM),
        scratch_shapes=[
            pltpu.VMEM((rows, bands, cols), BF16),
            pltpu.VMEM((rows, cols), jnp.int32),
            pltpu.SemaphoreType.DMA((2, 4)),
        ],
        compiler_params=params(),
        name="prep",
    )(*in_hbm(toa_bands, dark_mask))
    near_in = lax.ppermute(near_out, "along", swap_pairs(count, 1, 0))
    far_in = lax.ppermute(far_out, "along", swap_pairs(count, 1, 1))
    block = 256
    weights = (
        jax.ShapeDtypeStruct((levels_w, half, cols), F32),
        jax.ShapeDtypeStruct((half, cols), F32),
    )
    tables = [table.transpose(0, 1, 3, 2).reshape(-1, levels_a) for table in (lut_gain, lut_path, lut_albedo)]
    whole = jax.ShapeDtypeStruct((rows, cols), F32)
    whole_int = jax.ShapeDtypeStruct((rows, cols), jnp.int32)
    brought = [jax.ShapeDtypeStruct(table.shape, BF16) for table in tables] + [whole, whole_int, whole]
    *tables, vapours, classes, fracs, row_bands, taps = pl.pallas_call(
        early_kernel,
        out_shape=(
            *brought,
            jax.ShapeDtypeStruct((2, half, 3 * half), BF16),
            jax.ShapeDtypeStruct((1, kernel.shape[0]), F32),
        ),
        in_specs=[HBM] * 7,
        out_specs=(VMEM,) * 8,
        scratch_shapes=[pltpu.SemaphoreType.DMA((7,))],
        compiler_params=params(),
        name="early",
    )(*in_hbm(kernel[None, :], *tables, vapour, elev_class, elev_frac))

    def smooth_rows(flip, here, beside, incoming, *after):
        ext, edge = pl.pallas_call(
            functools.partial(vertical_kernel, flip),
            out_shape=(
                jax.ShapeDtypeStruct((2, 2, half, cols), BF16),
                jax.ShapeDtypeStruct((2, half, LANES), F32),
            ),
            in_specs=[VMEM] * (4 + len(after)),
            out_specs=(VMEM, VMEM),
            compiler_params=params(),
            name="vertical",
        )(row_bands, here, beside, incoming, *after)
        hats = pl.pallas_call(
            functools.partial(hats_kernel, flip),
            out_shape=weights,
            in_specs=[VMEM] * 4,
            out_specs=(VMEM, VMEM),
            compiler_params=params(),
            name="hats",
        )(vapours, classes, fracs, edge)
        return edge, lax.ppermute(edge, "across", swap_pairs(lax.axis_size("across"), 1, 0)), ext, *hats


    corrected = jax.ShapeDtypeStruct((half, bands, cols), BF16)
    sent, *near = smooth_rows(0, near_out, far_out, near_in)
    lut, col_bands = pl.pallas_call(
        functools.partial(tables_kernel, (bands, levels_e, levels_w, levels_a)),
        out_shape=(
            jax.ShapeDtypeStruct((6 * levels_e * bands, 2 * nodes), BF16),
            jax.ShapeDtypeStruct((2, block, block + 2 * LANES), BF16),
        ),
        in_specs=[VMEM] * 5,
        out_specs=(VMEM, VMEM),
        compiler_params=params(),
        name="tables",
    )(taps, *tables, sent)
    part = jax.ShapeDtypeStruct((SEG, bands, cols), BF16)
    near_first, near_pos = pl.pallas_call(
        functools.partial(near_kernel, levels_a),
        out_shape=(part, jax.ShapeDtypeStruct((half, cols), F32)),
        in_specs=[VMEM] * 8,
        out_specs=(VMEM, VMEM),
        compiler_params=params(),
        name="correct_near",
    )(col_bands, lut, *near, toa_bands, classes)
    near_corr = [near_first]
    sent, *far = smooth_rows(1, far_out, near_out, far_in, near_first)
    for first in range(SEG, half, SEG):
        near_corr.append(
            pl.pallas_call(
                functools.partial(next_kernel, first),
                out_shape=part,
                in_specs=[VMEM] * 7,
                out_specs=VMEM,
                compiler_params=params(),
                name="correct_next",
            )(lut, near[2], near[3], near_pos, toa_bands, classes, sent)
        )
    segments = rows // SEG
    slots = jax.ShapeDtypeStruct((CAP * SEG + 1, bands, cols), BF16)
    far_corr, *sides = pl.pallas_call(
        functools.partial(correct_far_kernel, levels_a),
        out_shape=(corrected,) + (slots,) * 4,
        in_specs=[HBM, HBM] + [VMEM] * (8 + len(near_corr)),
        out_specs=(VMEM,) * 5,
        scratch_shapes=[pltpu.VMEM((half, cols), F32)]
        + [pltpu.SMEM((2, segments), jnp.int32)] * 2
        + [pltpu.SemaphoreType.DMA((2,))],
        compiler_params=params(),
        name="correct_far",
    )(*in_hbm(routes.T, starts.T), col_bands, lut, *far, toa_bands, classes, *near_corr)
    moves = ((1, 0), (1, 1), (2, 0), (2, 1))
    got = [None] * 4
    for k in [0, 2, 1, 3]:
        step, offset = moves[k]
        got[k] = lax.ppermute(sides[k], "along", swap_pairs(count, step, offset))
    total = jax.ShapeDtypeStruct((rows, bands, cols), F32)
    counts = jax.ShapeDtypeStruct((rows, LANES), F32)
    acc, number = pl.pallas_call(
        own_kernel,
        out_shape=(total, counts),
        in_specs=[SMEM] + [VMEM] * (1 + len(near_corr)),
        out_specs=(VMEM, VMEM),
        compiler_params=params(),
        name="own",
    )(starts.T, *near_corr, far_corr)
    acc, number = pl.pallas_call(
        add_kernel,
        out_shape=(total, counts),
        in_specs=[VMEM] * 4,
        out_specs=(VMEM, VMEM),
        input_output_aliases={0: 0, 1: 1},
        compiler_params=params(),
        name="add",
    )(acc, number, got[0], got[2])
    _, out = pl.pallas_call(
        last_kernel,
        out_shape=(total, jax.ShapeDtypeStruct((rows, bands, cols), BF16)),
        in_specs=[VMEM] * 4,
        out_specs=(VMEM, HBM),
        scratch_shapes=[
            pltpu.VMEM((rows, LANES), F32),
            pltpu.VMEM((rows, bands, cols), BF16),
            pltpu.SemaphoreType.DMA((4,)),
        ],
        input_output_aliases={0: 0},
        compiler_params=params(),
        name="last",
    )(acc, number, got[1], got[3])
    return out[None]


def solution(mesh):
    in_specs = (
        P(("groups", "along"), None, "across"),
        P(("groups", "along"), "across"),
        P(("groups", "along"), "across"),
        P(("groups", "along"), "across"),
        P(("groups", "along"), "across"),
        P(),
        P(),
        P(),
        P(),
        P(("groups", "along"), None),
        P(("groups", "along"), None),
    )
    out_specs = P(("groups", "along"), None, None, "across")
    return jax.shard_map(body, mesh=mesh, in_specs=in_specs, out_specs=out_specs, check_vma=False)
```

```python
import functools

import jax
import jax.numpy as jnp
from jax import lax
from jax.experimental import pallas as pl
from jax.experimental.pallas import tpu as pltpu
from jax.sharding import PartitionSpec as P

SEG = 16
CAP = 2
LANES = 128

F32 = jnp.float32
BF16 = jnp.bfloat16
VMEM = pl.BlockSpec(memory_space=pltpu.VMEM)
HBM = pl.BlockSpec(memory_space=pltpu.HBM)
SMEM = pl.BlockSpec(memory_space=pltpu.SMEM)


def params(mib=24):
    return pltpu.CompilerParams(vmem_limit_bytes=mib * 1024 * 1024)


def swap_pairs(count, step, offset):
    pairs = []
    for i in range(count - step):
        if (i // step) % 2 == offset:
            pairs += [(i, i + step), (i + step, i)]
    return pairs


def in_hbm(*arrays):
    return [pltpu.with_memory_space_constraint(array, pltpu.HBM) for array in arrays]


def split_bf16(x):
    high = x.astype(BF16)
    return high, (x - high.astype(F32)).astype(BF16)


def prep_kernel(toa_ref, dark_ref, near_ref, far_ref, toa_in, dark_in, sems):
    rows = toa_in.shape[0]
    parts = 4
    size = rows // parts
    even = lax.axis_index("along") % 2 == 0
    copies = []
    for part in range(parts):
        at = pl.ds(part * size, size)
        copies.append(
            (
                pltpu.make_async_copy(toa_ref.at[at], toa_in.at[at], sems.at[0, part]),
                pltpu.make_async_copy(dark_ref.at[at], dark_in.at[at], sems.at[1, part]),
            )
        )
        for copy in copies[-1]:
            copy.start()
    for part in range(parts):
        for copy in copies[part]:
            copy.wait()
        at = slice(part * size, (part + 1) * size)
        to = slice(part % 2 * size, (part % 2 + 1) * size)
        into_near = even if part >= 2 else jnp.logical_not(even)
        dark = dark_in[at].astype(F32)
        lines = [(toa_in[at, band, :].astype(F32) * dark).astype(BF16) for band in (0, 2)]
        for flag, out_ref in ((into_near, near_ref), (jnp.logical_not(into_near), far_ref)):

            @pl.when(flag)
            def _():
                for field in range(2):
                    out_ref[field, to] = lines[field]


def store_bands(taps, out_ref, first):
    depth, width = out_ref.shape[1], out_ref.shape[2]
    taps = jnp.concatenate([taps, jnp.zeros((1, LANES - taps.shape[1]), F32)], axis=1)
    base = taps
    if width > LANES:
        base = jnp.concatenate([taps, jnp.zeros((1, width - LANES), F32)], axis=1)
    base = jnp.broadcast_to(base, (8, base.shape[1]))
    base = pltpu.roll(base, 0, 1, stride=1, stride_axis=0)
    for at in range(0, depth, 16):
        pair = [pltpu.roll(base, first + at + 8 * k, 1)[:, :width] for k in range(2)]
        high, low = split_bf16(jnp.concatenate(pair, axis=0))
        out_ref[0, at : at + 16] = high
        out_ref[1, at : at + 16] = low


def is_half(flip):
    return lax.axis_index("along") % 2 == flip


def vertical_kernel(flip, bands_ref, here_ref, beside_ref, in_ref, *rest):
    ext_ref, edge_ref = rest[-2:]
    lower = is_half(flip)
    left = lax.axis_index("across") == 0
    size = bands_ref.shape[1]
    matrix = jnp.concatenate([bands_ref[0], bands_ref[1]], axis=0)

    def field(index):
        beside, incoming = beside_ref[index], in_ref[index]
        return jnp.concatenate(
            [jnp.where(lower, beside, incoming), here_ref[index], jnp.where(lower, incoming, beside)], axis=0
        )

    def smooth(block):
        both = jnp.dot(matrix, block, preferred_element_type=F32)
        return both[:size] + both[size:]

    blue, red = field(0), field(1)
    dark = jnp.where(blue.astype(F32) > 0.0, 1.0, 0.0).astype(BF16)
    for index, value in enumerate((8.0 * (smooth(blue) - 0.5 * smooth(red)), smooth(dark))):
        edge_ref[index] = jnp.where(left, value[:, -LANES:], value[:, :LANES])
        high, low = split_bf16(value)
        ext_ref[0, index] = high
        ext_ref[1, index] = low


def store_table(array, out_ref, table, shape):
    bands, levels_e, levels_w, levels_a = shape
    nodes = levels_w * levels_a

    def iota(size, dim):
        return lax.broadcasted_iota(jnp.int32, size, dim)

    repeat = iota((levels_a, nodes), 1) % levels_a == iota((levels_a, nodes), 0)
    spread = jnp.dot(array, jnp.where(repeat, 1.0, 0.0).astype(BF16), preferred_element_type=F32)
    own = iota(spread.shape, 1) // levels_a == iota(spread.shape, 0) % levels_w
    spread = jnp.where(own, spread, 0.0).astype(BF16)
    size = (2 * bands * levels_e, spread.shape[0])
    row, source = iota(size, 0), iota(size, 1) // levels_w
    wanted = row % bands * levels_e + row // (2 * bands)
    for k in range(2):
        pick = (source == wanted) & (row // bands % 2 == k)
        part = jnp.dot(jnp.where(pick, 1.0, 0.0).astype(BF16), spread, preferred_element_type=F32)
        out_ref[table * size[0] : (table + 1) * size[0], k * nodes : (k + 1) * nodes] = part.astype(BF16)


def early_kernel(taps_ref, *refs):
    count = (len(refs) - 3) // 2
    sources, results, (rows_ref, taps_out_ref, sems) = refs[:count], refs[count : 2 * count], refs[2 * count :]
    pairs = [(taps_ref, taps_out_ref)] + list(zip(sources, results))
    copies = [pltpu.make_async_copy(source, into, sems.at[k]) for k, (source, into) in enumerate(pairs)]
    for copy in copies:
        copy.start()
    copies[0].wait()
    store_bands(taps_out_ref[...], rows_ref, rows_ref.shape[1] - 30)
    for copy in copies[1:]:
        copy.wait()


def tables_kernel(shape, taps_ref, gain_ref, path_ref, albedo_ref, *rest):
    lut_ref, cols_ref = rest[-2:]
    store_bands(taps_ref[...], cols_ref, LANES - 30)
    for number, table_ref in enumerate((gain_ref, path_ref, albedo_ref)):
        store_table(table_ref[...], lut_ref, number, shape)


def hats_kernel(flip, vapour_ref, class_ref, frac_ref, *rest):
    hat_ref, even_ref = rest[-2:]
    rows = even_ref.shape[0]
    here = pl.ds(pl.multiple_of(jnp.where(is_half(flip), rows, 0), rows), rows)
    vapour = vapour_ref[here]
    for w in range(hat_ref.shape[0]):
        hat_ref[w] = jnp.maximum(0.0, 1.0 - jnp.abs(vapour - float(w)))
    frac = frac_ref[here]
    even_ref[...] = jnp.where(class_ref[here] % 2 == 0, 1.0 - frac, frac)


def smooth_cols(bands_ref, edge_ref, ext_ref, pos_ref, levels_a):
    rows, cols = pos_ref.shape
    left = lax.axis_index("across") == 0
    block = bands_ref.shape[1]
    window = bands_ref.shape[2]
    lines = []
    for index in range(2):
        terms = split_bf16(edge_ref[index])
        for k in range(2):
            none = jnp.zeros_like(terms[k])
            lines.append((jnp.where(left, none, terms[k]), ext_ref[k, index], jnp.where(left, terms[k], none)))
    lines = [jnp.concatenate(line, axis=1) for line in (lines[0], lines[2], lines[1], lines[3])]
    windows = [slice(number * block, number * block + window) for number in range(cols // block)]
    contract = (((1,), (1,)), ((), ()))
    every = jnp.concatenate([line[:, at] for line in lines for at in windows], axis=0)
    full = lax.dot_general(every, bands_ref[0], contract, preferred_element_type=F32)
    rest = lax.dot_general(every[: every.shape[0] // 2], bands_ref[1], contract, preferred_element_type=F32)
    pieces = len(windows)
    for number in range(pieces):
        at = slice(number * block, (number + 1) * block)

        def part(array, line):
            return array[(line * pieces + number) * rows : (line * pieces + number + 1) * rows]

        weighted = part(full, 0) + (part(full, 2) + part(rest, 0))
        darkness = part(full, 1) + (part(full, 3) + part(rest, 1))
        aerosol = weighted / jnp.maximum(darkness, 1.0)
        pos_ref[:, at] = (levels_a - 1.0) / (1.0 + jnp.exp(-aerosol))


def correct_rows(flip, first, lut_ref, hat_ref, even_ref, pos_ref, toa_ref, class_ref, corr_ref):
    rows = corr_ref.shape[0]
    half, cols = pos_ref.shape
    base = pl.multiple_of(jnp.where(is_half(flip), half, 0) + first, rows)
    levels_w = hat_ref.shape[0]
    levels_a = lut_ref.shape[1] // (2 * levels_w)
    step = 256
    node_a = lax.broadcasted_iota(jnp.int32, (levels_a, step), 0).astype(F32)
    second = lax.broadcasted_iota(jnp.int32, (8, step), 0) >= 4
    lut = lut_ref[...]

    def pair(row, number):
        at = slice(number * step, (number + 1) * step)
        pieces = []
        for k in range(2):
            hat_a = jnp.maximum(0.0, 1.0 - jnp.abs(pos_ref[pl.ds(first + row + k, 1), at] - node_a)).astype(BF16)
            pieces += [
                hat_a * jnp.broadcast_to(hat_ref[w, pl.ds(first + row + k, 1), at], (levels_a, step)).astype(BF16) for w in range(levels_w)
            ]
        nodes = jnp.dot(lut, jnp.concatenate(pieces, axis=0), preferred_element_type=F32)

        def both(ref, begin):
            one, two = (jnp.broadcast_to(ref[pl.ds(begin + k, 1), at], (8, step)) for k in range(2))
            return jnp.where(second, two, one)

        level = both(class_ref, base + row)
        w_even = both(even_ref, first + row)
        below = [level < k for k in range(7)]

        def coefficient(table):
            node = [nodes[64 * table + 8 * k : 64 * table + 8 * k + 8] for k in range(8)]
            even = jnp.where(
                below[3], jnp.where(below[1], node[0], node[2]), jnp.where(below[5], node[4], node[6])
            )
            odd = jnp.where(
                below[4], jnp.where(below[2], node[1], node[3]), jnp.where(below[6], node[5], node[7])
            )
            return odd + w_even * (even - odd)

        toa = toa_ref[pl.ds(base + row, 2), :, at].astype(F32).reshape(8, step)
        scaled = coefficient(0) * toa - coefficient(1)
        surface = scaled / (1.0 + coefficient(2) * scaled)
        corr_ref[row, :, at] = surface[:4].astype(BF16)
        corr_ref[row + 1, :, at] = surface[4:].astype(BF16)

    group = 16

    def group_step(number, carry):
        for k in range(0, group, 2):
            for piece in range(cols // step):
                pair(number * group + k, piece)
        return carry

    lax.fori_loop(0, rows // group, group_step, 0)


def near_kernel(levels_a, bands_ref, lut_ref, edge_ref, ext_ref, hat_ref, even_ref, toa_ref, class_ref, corr_ref, pos_ref):
    smooth_cols(bands_ref, edge_ref, ext_ref, pos_ref, levels_a)
    correct_rows(0, 0, lut_ref, hat_ref, even_ref, pos_ref, toa_ref, class_ref, corr_ref)


def next_kernel(first, lut_ref, hat_ref, even_ref, pos_ref, toa_ref, class_ref, *rest):
    correct_rows(0, first, lut_ref, hat_ref, even_ref, pos_ref, toa_ref, class_ref, rest[-1])


def segment_list(near_refs, far_ref):
    each = far_ref.shape[0] // SEG
    shift = jnp.where(is_half(0), each, 0)
    near = [(shift + k, near_refs[k], 0) for k in range(each)]
    return near + [(each - shift + k, far_ref, k) for k in range(each)]


def correct_far_kernel(levels_a, routes_in_ref, starts_in_ref, *refs):
    near_refs, corr_ref, sides = refs[8:-9], refs[-9], refs[-8:-4]
    pos_ref, routes_ref, starts_ref, sems = refs[-4:]
    copies = [
        pltpu.make_async_copy(routes_in_ref, routes_ref, sems.at[0]),
        pltpu.make_async_copy(starts_in_ref, starts_ref, sems.at[1]),
    ]
    for copy in copies:
        copy.start()
    bands_ref, lut_ref, edge_ref, ext_ref, hat_ref, even_ref, toa_ref, class_ref = refs[:8]
    smooth_cols(bands_ref, edge_ref, ext_ref, pos_ref, levels_a)
    correct_rows(1, 0, lut_ref, hat_ref, even_ref, pos_ref, toa_ref, class_ref, corr_ref)
    for copy in copies:
        copy.wait()
    me = lax.axis_index("along")
    beside = 1 - 2 * (me % 2)
    beyond = 2 - 4 * ((me // 2) % 2)
    listed = segment_list(near_refs, corr_ref)
    band = lax.broadcasted_iota(jnp.int32, corr_ref.shape[1:], 0)
    for target, out_ref in zip((me + beside, me - beside, me + beyond, me - beyond), sides):
        count = jnp.int32(0)
        tags = [jnp.int32(0) for _ in range(CAP)]
        for segment, from_ref, place in listed:
            hit = routes_ref[1, segment] == target
            slot = count

            @pl.when(hit)
            def _():
                out_ref[pl.ds(slot * SEG, SEG)] = from_ref[place * SEG : (place + 1) * SEG]

            tag = jnp.where(hit, starts_ref[1, segment] + 1, 0)
            tags = [jnp.where(slot == k, tags[k] + tag, tags[k]) for k in range(CAP)]
            count = count + hit.astype(jnp.int32)
        line = jnp.zeros(band.shape, jnp.int32)
        for k in range(CAP):
            line = jnp.where(band == k, tags[k], line)
        out_ref[CAP * SEG] = line.astype(F32).astype(BF16)


def add_rows(acc_ref, start, from_ref, place):
    for row in range(SEG):
        acc_ref[start + row] = acc_ref[start + row] + from_ref[place * SEG + row].astype(F32)


def covers(rows, start):
    line = lax.broadcasted_iota(jnp.int32, (rows, LANES), 0)
    return jnp.where((line >= start) & (line < start + SEG), 1.0, 0.0)


def read_tags(side_refs):
    found = []
    for side_ref in side_refs:
        tags = side_ref[CAP * SEG, :, :LANES].astype(F32)
        band = lax.broadcasted_iota(jnp.int32, tags.shape, 0)
        for slot in range(CAP):
            found.append((jnp.max(jnp.where(band == slot, tags, 0.0)).astype(jnp.int32), side_ref, slot))
    return found


def add_sides(acc_ref, count, side_refs):
    found = read_tags(side_refs)
    for tag, side_ref, slot in found:
        start = jnp.maximum(tag - 1, 0)
        count = count + jnp.where(tag > 0, covers(count.shape[0], start), 0.0)

        @pl.when(tag > 0)
        def _():
            add_rows(acc_ref, start, side_ref, slot)

    return count


def own_kernel(starts_ref, *refs):
    far_ref, acc_ref, count_ref = refs[-3:]
    acc_ref[...] = jnp.zeros(acc_ref.shape, F32)
    count = jnp.zeros(count_ref.shape, F32)
    listed = segment_list(refs[:-3], far_ref)
    for segment, from_ref, place in listed:
        start = starts_ref[0, segment]
        count = count + covers(count.shape[0], start)
        add_rows(acc_ref, start, from_ref, place)
    count_ref[...] = count


def add_kernel(acc_in_ref, count_in_ref, side0_ref, side1_ref, acc_ref, count_ref):
    count_ref[...] = add_sides(acc_ref, count_in_ref[...], (side0_ref, side1_ref))


def last_kernel(acc_in_ref, count_in_ref, side0_ref, side1_ref, acc_ref, out_ref, inv_ref, line_ref, sems):
    count = add_sides(acc_ref, count_in_ref[...], (side0_ref, side1_ref))
    inv_ref[...] = 1.0 / jnp.maximum(count, 1.0)
    rows, bands, cols = line_ref.shape
    size = rows // 4
    copies = []
    for part in range(4):
        for row in range(part * size, (part + 1) * size):
            inverse = jnp.broadcast_to(inv_ref[row : row + 1, :], (bands, LANES))
            inverse = jnp.concatenate([inverse] * (cols // LANES), axis=1)
            line_ref[row] = (acc_ref[row] * inverse).astype(BF16)
        at = pl.ds(part * size, size)
        copies.append(pltpu.make_async_copy(line_ref.at[at], out_ref.at[at], sems.at[part]))
        copies[-1].start()
    for copy in copies:
        copy.wait()


def body(
    toa_bands,
    dark_mask,
    vapour,
    elev_class,
    elev_frac,
    kernel,
    lut_gain,
    lut_path,
    lut_albedo,
    routes,
    starts,
):
    rows, bands, cols = toa_bands.shape
    levels_e, levels_a, levels_w = lut_gain.shape[1:]
    nodes = levels_a * levels_w
    count = lax.axis_size("along")
    half = rows // 2
    fields = jax.ShapeDtypeStruct((2, half, cols), BF16)
    near_out, far_out = pl.pallas_call(
        prep_kernel,
        out_shape=(fields, fields),
        in_specs=[HBM, HBM],
        out_specs=(VMEM, VMEM),
        scratch_shapes=[
            pltpu.VMEM((rows, bands, cols), BF16),
            pltpu.VMEM((rows, cols), jnp.int32),
            pltpu.SemaphoreType.DMA((2, 4)),
        ],
        compiler_params=params(),
        name="prep",
    )(*in_hbm(toa_bands, dark_mask))
    near_in = lax.ppermute(near_out, "along", swap_pairs(count, 1, 0))
    far_in = lax.ppermute(far_out, "along", swap_pairs(count, 1, 1))
    block = 256
    weights = (
        jax.ShapeDtypeStruct((levels_w, half, cols), F32),
        jax.ShapeDtypeStruct((half, cols), F32),
    )
    tables = [table.transpose(0, 1, 3, 2).reshape(-1, levels_a) for table in (lut_gain, lut_path, lut_albedo)]
    whole = jax.ShapeDtypeStruct((rows, cols), F32)
    whole_int = jax.ShapeDtypeStruct((rows, cols), jnp.int32)
    brought = [jax.ShapeDtypeStruct(table.shape, BF16) for table in tables] + [whole, whole_int, whole]
    *tables, vapours, classes, fracs, row_bands, taps = pl.pallas_call(
        early_kernel,
        out_shape=(
            *brought,
            jax.ShapeDtypeStruct((2, half, 3 * half), BF16),
            jax.ShapeDtypeStruct((1, kernel.shape[0]), F32),
        ),
        in_specs=[HBM] * 7,
        out_specs=(VMEM,) * 8,
        scratch_shapes=[pltpu.SemaphoreType.DMA((7,))],
        compiler_params=params(),
        name="early",
    )(*in_hbm(kernel[None, :], *tables, vapour, elev_class, elev_frac))

    def smooth_rows(flip, here, beside, incoming, *after):
        ext, edge = pl.pallas_call(
            functools.partial(vertical_kernel, flip),
            out_shape=(
                jax.ShapeDtypeStruct((2, 2, half, cols), BF16),
                jax.ShapeDtypeStruct((2, half, LANES), F32),
            ),
            in_specs=[VMEM] * (4 + len(after)),
            out_specs=(VMEM, VMEM),
            compiler_params=params(),
            name="vertical",
        )(row_bands, here, beside, incoming, *after)
        hats = pl.pallas_call(
            functools.partial(hats_kernel, flip),
            out_shape=weights,
            in_specs=[VMEM] * 4,
            out_specs=(VMEM, VMEM),
            compiler_params=params(),
            name="hats",
        )(vapours, classes, fracs, after[0] if after else edge)
        return edge, lax.ppermute(edge, "across", swap_pairs(lax.axis_size("across"), 1, 0)), ext, *hats


    corrected = jax.ShapeDtypeStruct((half, bands, cols), BF16)
    sent, *near = smooth_rows(0, near_out, far_out, near_in)
    lut, col_bands = pl.pallas_call(
        functools.partial(tables_kernel, (bands, levels_e, levels_w, levels_a)),
        out_shape=(
            jax.ShapeDtypeStruct((6 * levels_e * bands, 2 * nodes), BF16),
            jax.ShapeDtypeStruct((2, block, block + 2 * LANES), BF16),
        ),
        in_specs=[VMEM] * 5,
        out_specs=(VMEM, VMEM),
        compiler_params=params(),
        name="tables",
    )(taps, *tables, sent)
    part = jax.ShapeDtypeStruct((SEG, bands, cols), BF16)
    near_first, near_pos = pl.pallas_call(
        functools.partial(near_kernel, levels_a),
        out_shape=(part, jax.ShapeDtypeStruct((half, cols), F32)),
        in_specs=[VMEM] * 8,
        out_specs=(VMEM, VMEM),
        compiler_params=params(),
        name="correct_near",
    )(col_bands, lut, *near, toa_bands, classes)
    near_corr = [near_first]
    sent, *far = smooth_rows(1, far_out, near_out, far_in, near_first)
    for first in range(SEG, half, SEG):
        near_corr.append(
            pl.pallas_call(
                functools.partial(next_kernel, first),
                out_shape=part,
                in_specs=[VMEM] * 7,
                out_specs=VMEM,
                compiler_params=params(),
                name="correct_next",
            )(lut, near[2], near[3], near_pos, toa_bands, classes, sent)
        )
    segments = rows // SEG
    slots = jax.ShapeDtypeStruct((CAP * SEG + 1, bands, cols), BF16)
    far_corr, *sides = pl.pallas_call(
        functools.partial(correct_far_kernel, levels_a),
        out_shape=(corrected,) + (slots,) * 4,
        in_specs=[HBM, HBM] + [VMEM] * (8 + len(near_corr)),
        out_specs=(VMEM,) * 5,
        scratch_shapes=[pltpu.VMEM((half, cols), F32)]
        + [pltpu.SMEM((2, segments), jnp.int32)] * 2
        + [pltpu.SemaphoreType.DMA((2,))],
        compiler_params=params(),
        name="correct_far",
    )(*in_hbm(routes.T, starts.T), col_bands, lut, *far, toa_bands, classes, *near_corr)
    moves = ((1, 0), (1, 1), (2, 0), (2, 1))
    got = [None] * 4
    for k in [0, 2, 1, 3]:
        step, offset = moves[k]
        got[k] = lax.ppermute(sides[k], "along", swap_pairs(count, step, offset))
    total = jax.ShapeDtypeStruct((rows, bands, cols), F32)
    counts = jax.ShapeDtypeStruct((rows, LANES), F32)
    acc, number = pl.pallas_call(
        own_kernel,
        out_shape=(total, counts),
        in_specs=[SMEM] + [VMEM] * (1 + len(near_corr)),
        out_specs=(VMEM, VMEM),
        compiler_params=params(),
        name="own",
    )(starts.T, *near_corr, far_corr)
    acc, number = pl.pallas_call(
        add_kernel,
        out_shape=(total, counts),
        in_specs=[VMEM] * 4,
        out_specs=(VMEM, VMEM),
        input_output_aliases={0: 0, 1: 1},
        compiler_params=params(),
        name="add",
    )(acc, number, got[0], got[2])
    _, out = pl.pallas_call(
        last_kernel,
        out_shape=(total, jax.ShapeDtypeStruct((rows, bands, cols), BF16)),
        in_specs=[VMEM] * 4,
        out_specs=(VMEM, HBM),
        scratch_shapes=[
            pltpu.VMEM((rows, LANES), F32),
            pltpu.VMEM((rows, bands, cols), BF16),
            pltpu.SemaphoreType.DMA((4,)),
        ],
        input_output_aliases={0: 0},
        compiler_params=params(),
        name="last",
    )(acc, number, got[1], got[3])
    return out[None]


def solution(mesh):
    in_specs = (
        P(("groups", "along"), None, "across"),
        P(("groups", "along"), "across"),
        P(("groups", "along"), "across"),
        P(("groups", "along"), "across"),
        P(("groups", "along"), "across"),
        P(),
        P(),
        P(),
        P(),
        P(("groups", "along"), None),
        P(("groups", "along"), None),
    )
    out_specs = P(("groups", "along"), None, None, "across")
    return jax.shard_map(body, mesh=mesh, in_specs=in_specs, out_specs=out_specs, check_vma=False)
```
